256 devices in a mesh: section: 4 (over x), replica: 64 (over y, z, core).
Axes of the slice: x: 4, y: 4, z: 8, core: 2. Of those that a mesh axis runs over, the one named last changes fastest.
Arguments:
- hidden_in: bfloat16 [2, 4096, 4096], P(None, 'replica'), may hold values from -16 to 16
- down_weight: bfloat16 [4, 4096, 128], P('section'), may hold values from -0.09375 to 0.09375
- up_weight: bfloat16 [4, 4096, 128], P('section'), may hold values from -0.5 to 0.5
- norm_gain: float32 [4, 4096], P('section'), may hold values from 0.1 to 1.9
- krylov_basis: float32 [6, 4, 2, 4096, 128], P(None, 'section', None, 'replica'), may hold values from -60 to 60, as said below
Outputs:
- new_vectors: float32 [2, 4, 2, 4096, 128], P(None, 'section', None, 'replica')
- hessenberg: float32 [2, 9], replicated
The draws below stay inside these ranges and needn't reach their ends.
Inputs may be any that keep to these rules, and one draw needn't show every extreme that they name: `krylov_basis`: krylov basis vectors, one per leading index.
All inputs are finite; a program needn't handle non-finite values.
Results may differ from the reference program's by a relative error of at most 0.00085.
Values may be sent and summed in bfloat16 or wider, within the bound.
A program may use at most 64 MiB of HBM per device.

```python
import jax
import jax.numpy as jnp
from jax import lax

D = 4096
R = 128
NMB = 2
KB = 6
ITERS = 2
LAYERS = 4
TOK_ALL = 4096
P_SIZE = 4194304


def draw_krylov_basis(key, part):
    key = jax.random.fold_in(key, 7)
    own_key, shared_key, column_key = jax.random.split(key, 3)
    full_shape = (KB, LAYERS, 2, D, R)
    own_part = jnp.clip(jax.random.normal(own_key, full_shape, jnp.float32), -4.0, 4.0)
    shared_part = jnp.clip(jax.random.normal(shared_key, full_shape[1:], jnp.float32), -4.0, 4.0)
    mixing = 0.5
    row_scale = jnp.power(10.0, jnp.arange(D, dtype=jnp.float32) / D)
    col_scale = jnp.power(10.0, jax.random.uniform(column_key, (R,), jnp.float32))
    return (own_part + mixing * shared_part[None]) * row_scale[:, None] * col_scale / 10.0


def spiked(values, key, source, target, blocks, factor):
    def block_of(axis_at):
        return (jnp.arange(values.shape[axis_at]) // (values.shape[axis_at] // blocks)).reshape((-1,) + (1,) * (values.ndim - 1 - axis_at))

    first = jax.random.permutation(key, blocks)[block_of(target)]
    far = (block_of(target) + blocks // 2) % blocks
    return jnp.where((block_of(source) == first) | (block_of(source) == far), factor * values, values)


def levels(key, extent, pieces, least, top_value):
    gain, own = 1.0, jax.random.fold_in(key, 6)
    for dim, parts in pieces:
        heights = jnp.exp(jax.random.uniform(jax.random.fold_in(own, dim), (parts,), jnp.float32, least / len(pieces), top_value / len(pieces)))
        gain = gain * jnp.repeat(heights, extent[dim] // parts).reshape([-1 if axis == dim else 1 for axis in range(len(extent))])
    return gain


def normal_values(stream_key, extent, width, reach, cuts=(), kind=jnp.bfloat16):
    values = jax.random.normal(stream_key, extent, jnp.float32) * width
    if len(cuts) > 0:
        values = levels(stream_key, extent, cuts, -0.22, 0.18) * values
    return jnp.clip(values, min=-reach, max=reach).astype(kind)


def heavy_noise(stream_key, shape, deviation, most, pieces, heavy, held_as=jnp.bfloat16):
    values = deviation * jax.random.normal(stream_key, shape, jnp.float32)
    if pieces:
        values = values * levels(stream_key, shape, pieces, -0.22, 0.18)
    return jnp.clip(spiked(values, jax.random.fold_in(stream_key, 3), *heavy), -most, most).astype(held_as)


def setup_inputs(seed: int = 0) -> dict:
    arg_keys = jax.random.split(jax.random.key(seed), 6)
    return {
        "hidden_in": heavy_noise(arg_keys[0], (NMB, TOK_ALL, D), 1.0, 16.0, ((1, 64),), (1, 2, 64, 4.0)),
        "down_weight": normal_values(arg_keys[1], (LAYERS, D, R), D ** -0.5, 0.09375, ((0, 4),)),
        "up_weight": normal_values(arg_keys[2], (LAYERS, D, R), R ** -0.5, 0.5, ((0, 4),)),
        "norm_gain": jnp.clip(1.0 + 0.18 * jax.random.normal(arg_keys[3], (LAYERS, D), jnp.float32), 0.1, 1.9),
        "krylov_basis": draw_krylov_basis(jax.random.fold_in(arg_keys[5], 71), 0),
    }


NORM_EPS = 1e-05
VEC_EPS = 1e-06

def primal_parts(rows_in, down_rows, gain_row):
    widened = rows_in.astype(jnp.float32)
    inv_rms = lax.rsqrt(lax.optimization_barrier(jnp.mean(widened * widened, axis=-1, keepdims=True)) + NORM_EPS)
    normed = (widened * inv_rms * gain_row).astype(jnp.bfloat16)
    pre_act = jnp.dot(normed, down_rows, preferred_element_type=jnp.float32)
    sig_val = jax.nn.sigmoid(pre_act)
    return (widened, inv_rms, normed, pre_act, sig_val)

def against_rows(left, right):
    return lax.dot_general(left, right, (((1,), (1,)), ((), ())), preferred_element_type=jnp.float32)

def over_tokens(left, right):
    return lax.dot_general(left, right, (((0,), (0,)), ((), ())), preferred_element_type=jnp.float32)

def tangent_part(widened, inv_rms, normed, pre_act, sig_val, hidden_act, tangent_in, down_rows, up_rows, gain_row, tan_down, tan_up):
    wide_tan = tangent_in.astype(jnp.float32)
    tan_rms = -(inv_rms * inv_rms * inv_rms) * lax.optimization_barrier(jnp.mean(widened * wide_tan, axis=-1, keepdims=True))
    tan_normed = ((wide_tan * inv_rms + widened * tan_rms) * gain_row).astype(jnp.bfloat16)
    tan_pre = jnp.dot(tan_normed, down_rows, preferred_element_type=jnp.float32) + jnp.dot(normed, tan_down, preferred_element_type=jnp.float32)
    sig_slope = sig_val + pre_act * sig_val * (1.0 - sig_val)
    tan_act = (tan_pre * sig_slope).astype(jnp.bfloat16)
    return (wide_tan + against_rows(tan_act, up_rows) + against_rows(hidden_act, tan_up)).astype(jnp.bfloat16)

def forward_pair(rows_in, tangent_in, down_rows, up_rows, gain_row, tan_down, tan_up):
    widened, inv_rms, normed, pre_act, sig_val = primal_parts(rows_in, down_rows, gain_row)
    hidden_act = (pre_act * sig_val).astype(jnp.bfloat16)
    result = (widened + against_rows(hidden_act, up_rows)).astype(jnp.bfloat16)
    tangent_out = tangent_part(widened, inv_rms, normed, pre_act, sig_val, hidden_act, tangent_in, down_rows, up_rows, gain_row, tan_down, tan_up)
    return (result, tangent_out)

def backward_part(rows_in, cotangent, down_rows, up_rows, gain_row):
    widened, inv_rms, normed, pre_act, sig_val = primal_parts(rows_in, down_rows, gain_row)
    hidden_act = (pre_act * sig_val).astype(jnp.bfloat16)
    grad_up = over_tokens(cotangent, hidden_act)
    back_act = jnp.dot(cotangent, up_rows, preferred_element_type=jnp.float32)
    sig_slope = sig_val + pre_act * sig_val * (1.0 - sig_val)
    back_pre = (back_act * sig_slope).astype(jnp.bfloat16)
    grad_down = over_tokens(normed, back_pre)
    back_norm = against_rows(back_pre, down_rows) * gain_row
    cube = inv_rms * inv_rms * inv_rms
    back_rows = cotangent.astype(jnp.float32) + inv_rms * back_norm - widened * cube * lax.optimization_barrier(jnp.mean(back_norm * widened, axis=-1, keepdims=True))
    return (back_rows.astype(jnp.bfloat16), grad_down, grad_up)

def curvature_product(hidden_in, down_weight, up_weight, norm_gain, vector):
    weight_scale = jnp.array([D ** (-0.5), R ** (-0.5)], dtype=jnp.float32).reshape(2, 1, 1)
    tangent_w = (vector * weight_scale).astype(jnp.bfloat16)
    grad_total = jnp.zeros((LAYERS, 2, D, R), jnp.float32)
    for micro_idx in range(NMB):
        rows_in = hidden_in[micro_idx]
        tangent_in = jnp.zeros_like(rows_in)
        saved_rows = []
        for layer_idx in range(LAYERS):
            saved_rows.append(rows_in)
            rows_in, tangent_in = forward_pair(rows_in, tangent_in, down_weight[layer_idx], up_weight[layer_idx], norm_gain[layer_idx], tangent_w[layer_idx, 0], tangent_w[layer_idx, 1])
        cotangent = tangent_in
        for layer_idx in reversed(range(LAYERS)):
            cotangent, grad_down, grad_up = backward_part(saved_rows[layer_idx], cotangent, down_weight[layer_idx], up_weight[layer_idx], norm_gain[layer_idx])
            grad_total = grad_total.at[layer_idx].add(jnp.stack([grad_down, grad_up]))
    return grad_total * weight_scale / (NMB * TOK_ALL)

def correlations(slot_bank, vector):
    return lax.optimization_barrier(jnp.sum(slot_bank * vector[None], axis=(1, 2, 3, 4))) / P_SIZE

def combine(coef, slot_bank):
    return jnp.tensordot(coef, slot_bank, axes=1, precision=lax.Precision.HIGHEST)

def reference(hidden_in, down_weight, up_weight, norm_gain, krylov_basis):
    slot_bank = jnp.concatenate([krylov_basis, jnp.zeros((ITERS,) + krylov_basis.shape[1:], jnp.float32)], axis=0)
    hess_rows = []
    for iter_idx in range(ITERS):
        image = curvature_product(hidden_in, down_weight, up_weight, norm_gain, slot_bank[KB - 1 + iter_idx])
        first_coef = correlations(slot_bank, image)
        cleaned = image - combine(first_coef, slot_bank)
        second_coef = correlations(slot_bank, cleaned)
        twice_clean = cleaned - combine(second_coef, slot_bank)
        length = jnp.sqrt(jnp.sum(twice_clean * twice_clean) / P_SIZE + VEC_EPS)
        slot_bank = slot_bank.at[KB + iter_idx].set(twice_clean / length)
        hess_rows.append(jnp.concatenate([first_coef + second_coef, length[None]]))
    return (slot_bank[KB:], jnp.stack(hess_rows))
```

```python
import functools

import jax
import jax.numpy as jnp
from jax import lax
from jax.experimental import pallas as pl
from jax.experimental.pallas import tpu as pltpu
from jax.sharding import PartitionSpec as P

ITERS = 2
NORM_EPS = 1e-05
VEC_EPS = 1e-06

YS, ZS, CS = 4, 8, 2
MESH = pl.DeviceIdType.MESH
F32 = jnp.float32
BF16 = jnp.bfloat16
VMEM_BYTES = 48 * 1024 * 1024


def dot(left, right):
    return jnp.dot(left, right, preferred_element_type=F32)


def dot_t(left, right):
    return lax.dot_general(left, right, (((1,), (1,)), ((), ())), preferred_element_type=F32)


def over_tokens(left, right):
    return lax.dot_general(left, right, (((0,), (0,)), ((), ())), preferred_element_type=F32)


def two_parts(wide):
    high = wide.astype(BF16)
    return high, (wide - high.astype(F32)).astype(BF16)


def place():
    sec, rep = lax.axis_index("section"), lax.axis_index("replica")
    core = lax.rem(rep, CS)
    zed = lax.rem(rep // CS, ZS)
    why = rep // (CS * ZS)
    return sec, why, zed, core


def device(sec, why, zed, core):
    return (sec, (why * ZS + zed) * CS + core)


def greet(partners):
    barrier = pltpu.get_barrier_semaphore()
    for partner in partners:
        pl.semaphore_signal(barrier, inc=1, device_id=partner, device_id_type=MESH)
    pl.semaphore_wait(barrier, len(partners))


def remote(src, dst, send_sem, recv_sem, partner):
    return pltpu.make_async_remote_copy(
        src_ref=src,
        dst_ref=dst,
        send_sem=send_sem,
        recv_sem=recv_sem,
        device_id=partner,
        device_id_type=MESH,
    )


def gather_body(out_ref, halves, place_now, sems):
    sec, why, zed, core = place_now
    ysend, yrecv, zsend, zrecv, csend, crecv, wsend, wrecv, vsend, vrecv, dsend, drecv = sems
    first, second = halves
    sibling = device(sec, why, zed, 1 - core)
    right = device(sec, why, lax.rem(zed + 1, ZS), core)
    left = device(sec, why, lax.rem(zed + ZS - 1, ZS), core)
    waits = []

    def z_at(step):
        return lax.rem(zed + step + ZS, ZS)

    def y_at(step):
        return lax.rem(why + step, YS)

    def bundle_a(z):
        return out_ref.at[first, :, z, core]

    def block_b(z):
        return out_ref.at[second, why, z, core]

    for step in range(1, YS):
        block = out_ref.at[first, why, zed, core]
        copy = remote(block, block, ysend.at[step - 1], yrecv.at[step - 1],
                      device(sec, y_at(step), zed, core))
        copy.start()
        waits.append(copy)

    def ring(view, send, recv, step, way):
        z = z_at(-way * (step - 1))
        idx = (step - 1) * 2 + (0 if way > 0 else 1)
        copy = remote(view(z), view(z), send.at[idx], recv.at[idx], right if way > 0 else left)
        copy.start()
        waits.append(copy)

    def ring_arrived(view, send, recv, step, way):
        z = z_at(-way * step)
        idx = (step - 1) * 2 + (0 if way > 0 else 1)
        remote(view(z), view(z), send.at[idx], recv.at[idx], right).wait_recv()
        return z

    def to_sibling_a(z, idx):
        copy = remote(bundle_a(z), bundle_a(z), csend.at[idx], crecv.at[idx], sibling)
        copy.start()
        waits.append(copy)

    ring(block_b, wsend, wrecv, 1, 1)
    ring(block_b, wsend, wrecv, 1, -1)
    for step in range(1, YS):
        block = out_ref.at[first, y_at(YS - step), zed, core]
        remote(block, block, ysend.at[step - 1], yrecv.at[step - 1], sibling).wait_recv()
    ring(bundle_a, zsend, zrecv, 1, 1)
    ring(bundle_a, zsend, zrecv, 1, -1)
    to_sibling_a(zed, 0)
    count = 1
    half = ZS // 2
    for step in range(1, half + 1):
        for way in (1, -1):
            if way < 0 and step == half:
                continue
            ring_arrived(block_b, wsend, wrecv, step, way)
            if step + 1 < half or (step + 1 == half and way > 0):
                ring(block_b, wsend, wrecv, step + 1, way)
    for step in range(1, YS):
        bundle = out_ref.at[second, why, :, core]
        copy = remote(bundle, bundle, vsend.at[step - 1], vrecv.at[step - 1],
                      device(sec, y_at(step), zed, core))
        copy.start()
        waits.append(copy)
    bundle = out_ref.at[second, why, :, core]
    copy = remote(bundle, bundle, dsend.at[0], drecv.at[0], sibling)
    copy.start()
    waits.append(copy)
    for step in range(1, half + 1):
        for way in (1, -1):
            if way < 0 and step == half:
                continue
            z = ring_arrived(bundle_a, zsend, zrecv, step, way)
            if step + 1 < half or (step + 1 == half and way > 0):
                ring(bundle_a, zsend, zrecv, step + 1, way)
            to_sibling_a(z, count)
            count += 1
    for step in range(1, YS):
        y = y_at(YS - step)
        bundle = out_ref.at[second, y, :, core]
        remote(bundle, bundle, vsend.at[step - 1], vrecv.at[step - 1], sibling).wait_recv()
        copy = remote(bundle, bundle, dsend.at[step], drecv.at[step], sibling)
        copy.start()
        waits.append(copy)
    order = [0]
    for step in range(1, half + 1):
        order.append(-step)
        if step < half:
            order.append(step)
    for idx, step in enumerate(order):
        block = out_ref.at[first, :, z_at(step), 1 - core]
        remote(block, block, csend.at[idx], crecv.at[idx], sibling).wait_recv()
    for step in range(YS):
        block = out_ref.at[second, y_at((YS - step) % YS), :, 1 - core]
        remote(block, block, dsend.at[step], drecv.at[step], sibling).wait_recv()
    for copy in waits:
        copy.wait_send()


GATHER_SEMS = (
    [pltpu.SemaphoreType.DMA((YS - 1,))] * 2
    + [pltpu.SemaphoreType.DMA((ZS,))] * 2
    + [pltpu.SemaphoreType.DMA((ZS,))] * 2
    + [pltpu.SemaphoreType.DMA((ZS,))] * 2
    + [pltpu.SemaphoreType.DMA((YS - 1,))] * 2
    + [pltpu.SemaphoreType.DMA((YS,))] * 2
)


def gather_partners(place_now):
    sec, why, zed, core = place_now
    partners = [device(sec, lax.rem(why + step, YS), zed, core) for step in range(1, YS)]
    partners.append(device(sec, why, lax.rem(zed + 1, ZS), core))
    partners.append(device(sec, why, lax.rem(zed + ZS - 1, ZS), core))
    partners.append(device(sec, why, zed, 1 - core))
    return partners


def section_partners(place_now, count):
    sec, why, zed, core = place_now
    return [device(lax.rem(sec + step, count), why, zed, core) for step in range(1, count)]


def vector_kernel(sections, shard_ref, out_ref, ups_ref, local, xsend, xrecv, *sems):
    place_now = place()
    sec, why, zed, core = place_now
    others = section_partners(place_now, sections)
    greet(others + gather_partners(place_now))
    blocks = shard_ref.shape[0]
    mine = out_ref.at[:, why, zed, core]
    own = pltpu.make_async_copy(shard_ref, mine, local.at[0])
    own.start()
    keep = pltpu.make_async_copy(shard_ref.at[blocks - 1], ups_ref.at[sec], local.at[1])
    keep.start()
    sends = []
    for step in range(1, sections):
        copy = remote(shard_ref.at[blocks - 1], ups_ref.at[sec], xsend.at[step - 1],
                      xrecv.at[step - 1], others[step - 1])
        copy.start()
        sends.append(copy)
    own.wait()
    half = blocks // 2
    gather_body(out_ref, (pl.ds(0, half), pl.ds(half, blocks - half)), place_now, sems)
    keep.wait()
    for step in range(1, sections):
        source = lax.rem(sec + sections - step, sections)
        remote(shard_ref.at[blocks - 1], ups_ref.at[source], xsend.at[step - 1],
               xrecv.at[step - 1], others[0]).wait_recv()
    for copy in sends:
        copy.wait_send()


def gather_vector(shard, sections, collective_id):
    blocks, rows, lanes = shard.shape
    return pl.pallas_call(
        functools.partial(vector_kernel, sections),
        out_shape=(
            jax.ShapeDtypeStruct((blocks, YS, ZS, CS, rows, lanes), shard.dtype),
            jax.ShapeDtypeStruct((sections, rows, lanes), shard.dtype),
        ),
        in_specs=[pl.BlockSpec(memory_space=pltpu.VMEM)],
        out_specs=(pl.BlockSpec(memory_space=pl.ANY), pl.BlockSpec(memory_space=pl.ANY)),
        scratch_shapes=[
            pltpu.SemaphoreType.DMA((2,)),
            pltpu.SemaphoreType.DMA((sections - 1,)),
            pltpu.SemaphoreType.DMA((sections - 1,)),
        ] + GATHER_SEMS,
        compiler_params=pltpu.CompilerParams(collective_id=collective_id, has_side_effects=True),
    )(shard)


def first_kernel(sections, shard_ref, weight_ref, gain_ref, out_ref, ups_ref, gains_ref,
                 local, xsend, xrecv, *sems):
    place_now = place()
    sec, why, zed, core = place_now
    others = section_partners(place_now, sections)
    greet(others + gather_partners(place_now))
    pairs = out_ref.shape[0]

    def mine(layer):
        return out_ref.at[pl.ds(2 * layer, 2), why, zed, core]

    locals_ = [
        pltpu.make_async_copy(shard_ref, mine(sec), local.at[0]),
        pltpu.make_async_copy(shard_ref.at[1], ups_ref.at[sec], local.at[1]),
        pltpu.make_async_copy(gain_ref, gains_ref.at[sec], local.at[2]),
    ]
    for copy in locals_:
        copy.start()
    sends = []
    for step in range(1, sections):
        for idx, (src, dst) in enumerate((
            (weight_ref, mine(sec)),
            (shard_ref.at[1], ups_ref.at[sec]),
            (gain_ref, gains_ref.at[sec]),
        )):
            copy = remote(src, dst, xsend.at[step - 1, idx], xrecv.at[step - 1, idx],
                          others[step - 1])
            copy.start()
            sends.append(copy)
    locals_[0].wait()
    for step in range(1, sections):
        source = lax.rem(sec + sections - step, sections)
        remote(weight_ref, mine(source), xsend.at[step - 1, 0], xrecv.at[step - 1, 0],
               others[0]).wait_recv()
    half = pairs // 2
    gather_body(out_ref, (pl.ds(0, half), pl.ds(half, pairs - half)), place_now, sems)
    for copy in locals_[1:]:
        copy.wait()
    for step in range(1, sections):
        source = lax.rem(sec + sections - step, sections)
        remote(shard_ref.at[1], ups_ref.at[source], xsend.at[step - 1, 1],
               xrecv.at[step - 1, 1], others[0]).wait_recv()
        remote(gain_ref, gains_ref.at[source], xsend.at[step - 1, 2],
               xrecv.at[step - 1, 2], others[0]).wait_recv()
    for copy in sends:
        copy.wait_send()


def gather_first(shard, weight_rows, gain, sections, collective_id):
    blocks, rows, lanes = shard.shape
    hbm = pl.BlockSpec(memory_space=pl.ANY)
    vmem = pl.BlockSpec(memory_space=pltpu.VMEM)
    return pl.pallas_call(
        functools.partial(first_kernel, sections),
        out_shape=(
            jax.ShapeDtypeStruct((blocks * sections, YS, ZS, CS, rows, lanes), shard.dtype),
            jax.ShapeDtypeStruct((sections, rows, lanes), shard.dtype),
            jax.ShapeDtypeStruct((sections,) + gain.shape, gain.dtype),
        ),
        in_specs=[vmem, vmem, vmem],
        out_specs=(hbm, hbm, hbm),
        scratch_shapes=[
            pltpu.SemaphoreType.DMA((3,)),
            pltpu.SemaphoreType.DMA((sections - 1, 3)),
            pltpu.SemaphoreType.DMA((sections - 1, 3)),
        ] + GATHER_SEMS,
        compiler_params=pltpu.CompilerParams(collective_id=collective_id, has_side_effects=True),
    )(shard, weight_rows, gain)


def rows_kernel(shard_ref, out_ref, local, *sems):
    place_now = place()
    sec, why, zed, core = place_now
    greet(gather_partners(place_now))
    blocks = shard_ref.shape[0]
    own = pltpu.make_async_copy(shard_ref, out_ref.at[:, why, zed, core], local)
    own.start()
    own.wait()
    half = blocks // 2
    gather_body(out_ref, (pl.ds(0, half), pl.ds(half, blocks - half)), place_now, sems)


def gather_rows(shard, collective_id):
    blocks, rows, lanes = shard.shape
    return pl.pallas_call(
        rows_kernel,
        out_shape=jax.ShapeDtypeStruct((blocks, YS, ZS, CS, rows, lanes), shard.dtype),
        in_specs=[pl.BlockSpec(memory_space=pltpu.VMEM)],
        out_specs=pl.BlockSpec(memory_space=pl.ANY),
        scratch_shapes=[pltpu.SemaphoreType.DMA] + GATHER_SEMS,
        compiler_params=pltpu.CompilerParams(collective_id=collective_id, has_side_effects=True),
    )(shard)


def recurrence(tan_base, back_base, pre_act, slope, inv_rms, row_up, up_up, up_down, full_d):
    layers = len(tan_base)
    tan_act = []
    for layer in range(layers):
        tan_pre = tan_base[layer]
        if layer > 0:
            moved = sum(dot(tan_act[k], up_down[k][layer][0]) + dot(tan_act[k], up_down[k][layer][1])
                        for k in range(layer))
            along = sum(jnp.sum(tan_act[k].astype(F32) * row_up[layer][k], axis=-1, keepdims=True)
                        for k in range(layer))
            inv = inv_rms[layer]
            tan_pre = tan_pre + inv * moved - (inv * inv * (1.0 / full_d)) * along * pre_act[layer]
        tan_act.append((tan_pre * slope[layer]).astype(BF16))
    every = jnp.concatenate(tan_act, axis=1)
    back_all = dot(every, up_up[0]) + dot(every, up_up[1])
    back_pre, moved_back, pull = {}, {}, {}
    for layer in reversed(range(layers)):
        back_act = back_base[layer] + back_all[:, layer * 128:(layer + 1) * 128]
        for k in range(layer + 1, layers):
            back_act = back_act + dot_t(moved_back[k], up_down[layer][k][0])
            back_act = back_act + dot_t(moved_back[k], up_down[layer][k][1])
            back_act = back_act - pull[k] * row_up[k][layer]
        piece = (back_act * slope[layer]).astype(BF16)
        wide = piece.astype(F32)
        inv = inv_rms[layer]
        back_pre[layer] = piece
        moved_back[layer] = (wide * inv).astype(BF16)
        pull[layer] = inv * inv * (1.0 / full_d) * jnp.sum(wide * pre_act[layer], axis=-1, keepdims=True)
    return tan_act, [back_pre[layer] for layer in range(layers)]


def token_kernel(sections, full_d, pay_ref, pre_ref, slope_ref, inv_ref, rowup_ref, uuh_ref, uul_ref,
                 udh_ref, udl_ref, out_ref, arrive, result, xsend, xrecv, ysend, yrecv):
    place_now = place()
    sec = place_now[0]
    others = section_partners(place_now, sections)
    greet(others)
    first = []
    for step in range(1, sections):
        target = lax.rem(sec + step, sections)
        copy = remote(pay_ref.at[target], arrive.at[step - 1], xsend.at[step - 1],
                      xrecv.at[step - 1], others[step - 1])
        copy.start()
        first.append(copy)
    total = pay_ref[sec].astype(F32)
    for copy in first:
        copy.wait()
    for step in range(sections - 1):
        total = total + arrive[step].astype(F32)
    layers = sections

    def block(idx):
        return total[:, idx * 128:(idx + 1) * 128]

    row_up = {}
    idx = 0
    for layer in range(layers):
        for k in range(layer):
            row_up.setdefault(layer, {})[k] = rowup_ref[idx]
            idx += 1
    up_down = {k: {} for k in range(layers)}
    idx = 0
    for layer in range(layers):
        for k in range(layer):
            up_down[k][layer] = (udh_ref[idx], udl_ref[idx])
            idx += 1
    tan_act, back_pre = recurrence(
        [block(layer) for layer in range(layers)],
        [block(layers + layer) for layer in range(layers)],
        [pre_ref[layer] for layer in range(layers)],
        [slope_ref[layer] for layer in range(layers)],
        [inv_ref[layer] for layer in range(layers)],
        row_up,
        (uuh_ref[...], uul_ref[...]),
        up_down,
        full_d,
    )
    result[...] = jnp.concatenate(tan_act + back_pre, axis=1)
    out_ref[sec] = result[...]
    second = []
    for step in range(1, sections):
        copy = remote(result, out_ref.at[sec], ysend.at[step - 1], yrecv.at[step - 1],
                      others[step - 1])
        copy.start()
        second.append(copy)
    for copy in second:
        copy.wait()


def run_tokens(pay, consts, sections, full_d, collective_id):
    vmem = pl.BlockSpec(memory_space=pltpu.VMEM)
    tok, width = pay.shape[1:]
    return pl.pallas_call(
        functools.partial(token_kernel, sections, full_d),
        out_shape=jax.ShapeDtypeStruct(pay.shape, BF16),
        in_specs=[vmem] * (1 + len(consts)),
        out_specs=vmem,
        scratch_shapes=[
            pltpu.VMEM((sections - 1, tok, width), BF16),
            pltpu.VMEM((tok, width), BF16),
        ] + [pltpu.SemaphoreType.DMA((sections - 1,))] * 4,
        compiler_params=pltpu.CompilerParams(
            collective_id=collective_id, has_side_effects=True, vmem_limit_bytes=VMEM_BYTES),
    )(pay, *consts)


def reduce_kernel(a_ref, b_ref, outa_ref, outb_ref, swap_a, swap_b, left_in, right_in, y_a, y_b, z_b,
                  csa, cra, csb, crb, ls, lr, rs, rr, yas, yar, ybs, ybr, zbs, zbr):
    place_now = place()
    sec, why, zed, core = place_now
    sibling = device(sec, why, zed, 1 - core)

    def z_at(step):
        return lax.rem(zed + step + ZS, ZS)

    def y_at(step):
        return lax.rem(why + step + YS, YS)

    z_dev = [device(sec, why, z_at(step), core) for step in range(ZS)]
    y_dev = [device(sec, y_at(step), zed, core) for step in range(YS)]
    right, left = z_dev[1], z_dev[ZS - 1]
    greet([sibling] + z_dev[1:] + y_dev[1:])
    waits = []

    def go(copy):
        copy.start()
        waits.append(copy)

    half = ZS // 2
    a_order = [half]
    for step in range(1, half):
        a_order += [half - step, -(half - step)]
    a_order.append(0)
    b_order = [2, 1, 3, 0]
    pos_a = {(step + ZS) % ZS: idx for idx, step in enumerate(a_order)}
    pos_b = {step: idx for idx, step in enumerate(b_order)}

    def swap_copy_a(step):
        idx = pos_a[step % ZS]
        z = z_at(step)
        return remote(a_ref.at[:, z, 1 - core], swap_a.at[z], csa.at[idx], cra.at[idx], sibling)

    def swap_copy_b(step):
        idx = pos_b[step]
        y = y_at(step)
        return remote(b_ref.at[y, :, 1 - core], swap_b.at[y], csb.at[idx], crb.at[idx], sibling)

    for idx in range(ZS):
        go(swap_copy_a(a_order[idx]))
        if idx % 2 == 1:
            go(swap_copy_b(b_order[idx // 2]))

    def chip_sum_a(step):
        swap_copy_a(step).wait_recv()
        z = z_at(step)
        return swap_a[z] + a_ref[:, z, core]

    def chip_sum_b(step):
        swap_copy_b(step).wait_recv()
        y = y_at(step)
        return swap_b[y] + b_ref[y, :, core]

    def left_copy(step):
        z = z_at(step - half - 1)
        return remote(swap_a.at[z], left_in.at[step - 1], ls.at[step - 1], lr.at[step - 1], left)

    def right_copy(step):
        z = z_at(half - step)
        return remote(swap_a.at[z], right_in.at[step - 1], rs.at[step - 1], rr.at[step - 1], right)

    def y_copy_b(step):
        return remote(swap_b.at[y_at(step)], y_b.at[step - 1], ybs.at[step - 1], ybr.at[step - 1],
                      y_dev[step])

    def send_b(step):
        swap_b[y_at(step)] = chip_sum_b(step)
        go(y_copy_b(step))

    for step in range(1, half + 1):
        value = chip_sum_a(step - half - 1)
        if step > 1:
            left_copy(step - 1).wait_recv()
            value = value + left_in[step - 2]
        swap_a[z_at(step - half - 1)] = value
        go(left_copy(step))
        if step < half:
            value = chip_sum_a(half - step)
            if step > 1:
                right_copy(step - 1).wait_recv()
                value = value + right_in[step - 2]
            swap_a[z_at(half - step)] = value
            go(right_copy(step))
            send_b(b_order[step - 1])

    mine_a = chip_sum_a(0)
    mine_b = chip_sum_b(0)
    right_copy(half - 1).wait_recv()
    mine_a = mine_a + right_in[half - 2]
    left_copy(half).wait_recv()
    swap_a[zed] = mine_a + left_in[half - 1]

    def y_copy_a(step):
        return remote(swap_a.at[zed, y_at(step)], y_a.at[step - 1], yas.at[step - 1], yar.at[step - 1],
                      y_dev[step])

    for step in range(1, YS):
        go(y_copy_a(step))
    for step in range(1, YS):
        y_copy_b(step).wait_recv()
        mine_b = mine_b + y_b[step - 1]
    swap_b[why] = mine_b

    def z_copy_b(step):
        return remote(swap_b.at[why, z_at(step)], z_b.at[step - 1], zbs.at[step - 1], zbr.at[step - 1],
                      z_dev[step])

    for step in range(1, ZS):
        go(z_copy_b(step))
    value = swap_a[zed, why]
    for step in range(1, YS):
        y_copy_a(step).wait_recv()
        value = value + y_a[step - 1]
    outa_ref[...] = value
    value = swap_b[why, zed]
    for step in range(1, ZS):
        z_copy_b(step).wait_recv()
        value = value + z_b[step - 1]
    outb_ref[...] = value
    for copy in waits:
        copy.wait_send()


def reduce_rows(part_a, part_b, collective_id):
    rows_a, rows_b = part_a.shape[3], part_b.shape[3]
    vmem = pl.BlockSpec(memory_space=pltpu.VMEM)
    dma = pltpu.SemaphoreType.DMA
    half = ZS // 2
    return pl.pallas_call(
        reduce_kernel,
        out_shape=(
            jax.ShapeDtypeStruct((rows_a, 128), F32),
            jax.ShapeDtypeStruct((rows_b, 128), F32),
        ),
        in_specs=[vmem, vmem],
        out_specs=(vmem, vmem),
        scratch_shapes=[
            pltpu.VMEM((ZS, YS, rows_a, 128), F32),
            pltpu.VMEM((YS, ZS, rows_b, 128), F32),
            pltpu.VMEM((half, YS, rows_a, 128), F32),
            pltpu.VMEM((half - 1, YS, rows_a, 128), F32),
            pltpu.VMEM((YS - 1, rows_a, 128), F32),
            pltpu.VMEM((YS - 1, ZS, rows_b, 128), F32),
            pltpu.VMEM((ZS - 1, rows_b, 128), F32),
            dma((ZS,)), dma((ZS,)),
            dma((YS,)), dma((YS,)),
            dma((half,)), dma((half,)),
            dma((half - 1,)), dma((half - 1,)),
            dma((YS - 1,)), dma((YS - 1,)),
            dma((YS - 1,)), dma((YS - 1,)),
            dma((ZS - 1,)), dma((ZS - 1,)),
        ],
        compiler_params=pltpu.CompilerParams(
            collective_id=collective_id, has_side_effects=True, vmem_limit_bytes=VMEM_BYTES),
    )(part_a, part_b)


def sum_kernel(sections, vec_ref, out_ref, near, far, half_sum, ns, nr, fs, fr):
    sec, why, zed, core = place()
    inner = ZS * CS
    outer = sections * YS
    here = zed * CS + core
    there = sec * YS + why

    def near_dev(step):
        other = lax.rem(here + step, inner)
        return (sec, why * inner + other)

    def far_dev(step):
        other = lax.rem(there + step, outer)
        return (other // YS, lax.rem(other, YS) * inner + here)

    near_all = [near_dev(step) for step in range(1, inner)]
    far_all = [far_dev(step) for step in range(1, outer)]
    greet(near_all + far_all)
    sends = []
    for step in range(1, inner):
        copy = remote(vec_ref, near.at[here], ns.at[step - 1], nr.at[step - 1], near_all[step - 1])
        copy.start()
        sends.append(copy)
    near[here] = vec_ref[...]
    for step in range(1, inner):
        source = lax.rem(here + inner - step, inner)
        remote(vec_ref, near.at[source], ns.at[step - 1], nr.at[step - 1], near_all[0]).wait_recv()
    half_sum[...] = jnp.sum(near[...], axis=0)
    for step in range(1, outer):
        copy = remote(half_sum, far.at[there], fs.at[step - 1], fr.at[step - 1], far_all[step - 1])
        copy.start()
        sends.append(copy)
    far[there] = half_sum[...]
    for step in range(1, outer):
        source = lax.rem(there + outer - step, outer)
        remote(half_sum, far.at[source], fs.at[step - 1], fr.at[step - 1], far_all[0]).wait_recv()
    out_ref[...] = jnp.sum(far[...], axis=0)
    for copy in sends:
        copy.wait_send()


def sum_all(vec, sections, collective_id):
    vmem = pl.BlockSpec(memory_space=pltpu.VMEM)
    inner, outer = ZS * CS, sections * YS
    dma = pltpu.SemaphoreType.DMA
    return pl.pallas_call(
        functools.partial(sum_kernel, sections),
        out_shape=jax.ShapeDtypeStruct(vec.shape, F32),
        in_specs=[vmem],
        out_specs=vmem,
        scratch_shapes=[
            pltpu.VMEM((inner,) + vec.shape, F32),
            pltpu.VMEM((outer,) + vec.shape, F32),
            pltpu.VMEM(vec.shape, F32),
            dma((inner - 1,)), dma((inner - 1,)),
            dma((outer - 1,)), dma((outer - 1,)),
        ],
        compiler_params=pltpu.CompilerParams(collective_id=collective_id, has_side_effects=True),
    )(vec)


def primal(rows, downs, ups, gains):
    layers = downs.shape[0]
    out = []
    for layer in range(layers):
        widened = rows.astype(F32)
        inv_rms = lax.rsqrt(jnp.mean(widened * widened, axis=-1, keepdims=True) + NORM_EPS)
        normed = (widened * inv_rms * gains[layer]).astype(BF16)
        pre_act = dot(normed, downs[layer])
        sig_val = jax.nn.sigmoid(pre_act)
        hidden_act = (pre_act * sig_val).astype(BF16)
        slope = sig_val + pre_act * sig_val * (1.0 - sig_val)
        out.append((rows, inv_rms, normed, pre_act, slope, hidden_act))
        if layer + 1 < layers:
            rows = (widened + dot_t(hidden_act, ups[layer])).astype(BF16)
    return out


def pick(items, sec):
    return lax.dynamic_index_in_dim(jnp.stack(items), sec, 0, keepdims=False)


def per_device(hidden_in, down_weight, up_weight, norm_gain, krylov_basis):
    layers = lax.axis_size("section")
    sec = lax.axis_index("section")
    rep = lax.axis_index("replica")
    micro, tok, full_d = hidden_in.shape
    rank = down_weight.shape[2]
    tokens = micro * tok
    part = tokens // layers
    basis = krylov_basis[:, 0]
    base_count, _, own_rows, _ = basis.shape
    scales = jnp.array([full_d ** -0.5, rank ** -0.5], F32).reshape(2, 1, 1)
    param_count = float(layers * 2 * full_d * rank)

    weight_rows = jnp.stack([
        lax.dynamic_slice_in_dim(down_weight[0], rep * own_rows, own_rows, 0),
        lax.dynamic_slice_in_dim(up_weight[0], rep * own_rows, own_rows, 0),
    ])
    shard = (basis[base_count - 1] * scales).astype(BF16)
    gathered, up_shards, gains = gather_first(
        shard, weight_rows, norm_gain.reshape(full_d // 128, 128), layers, 1)
    gathered = gathered.reshape(layers, 2, full_d, rank)
    vector = lax.dynamic_index_in_dim(gathered, sec, 0, keepdims=False)
    weights = lax.dynamic_update_index_in_dim(
        gathered, jnp.stack([down_weight[0], up_weight[0]]), sec, 0)
    downs, ups = weights[:, 0], weights[:, 1]
    gains = gains.reshape(layers, 1, full_d)

    rows0 = hidden_in.reshape(tokens, full_d)
    state = primal(rows0, downs, ups, gains)
    all_rows = [item[0] for item in state]
    inv_rms = [item[1] for item in state]
    pre_act = [item[3] for item in state]
    own_normed = pick([item[2] for item in state], sec)
    hidden = [item[5] for item in state]
    own_hidden = pick(hidden, sec)
    hidden_cat = jnp.concatenate(hidden, axis=1)

    def own_part(array):
        return lax.dynamic_slice_in_dim(array, sec * part, part, 0)

    up_cat = jnp.concatenate([ups[layer] for layer in range(layers)], axis=1)
    up_up = two_parts(over_tokens(up_cat, up_cat))
    up_down = []
    row_up = []
    for layer in range(layers):
        for k in range(layer):
            high, low = two_parts(ups[k].astype(F32) * gains[layer].reshape(full_d, 1))
            up_down.append(two_parts(
                over_tokens(high, downs[layer]) + over_tokens(low, downs[layer])))
            row_up.append(dot(own_part(all_rows[layer]), ups[k]))
    consts = (
        jnp.stack([own_part(item) for item in pre_act]),
        jnp.stack([own_part(item[4]) for item in state]),
        jnp.stack([jnp.broadcast_to(own_part(item), (part, 128)) for item in inv_rms]),
        jnp.stack(row_up),
        up_up[0],
        up_up[1],
        jnp.stack([item[0] for item in up_down]),
        jnp.stack([item[1] for item in up_down]),
    )
    own_gram = over_tokens(hidden_cat, own_hidden)

    slots = basis
    gram_rows = jnp.einsum("kabc,jabc->kj", basis, basis, precision=lax.Precision.HIGHEST)
    gram = None
    norm_factor = 1.0 / (tokens * lax.axis_size("replica"))
    hess, new_vectors = [], []
    hidden_gram = None
    for it in range(ITERS):
        tan_down, tan_up = vector[0], vector[1]
        base = dot(own_normed, tan_down)
        spread = dot_t(own_hidden, tan_up)
        spread_up = dot(spread.astype(BF16), up_cat)
        terms = []
        for layer in range(layers):
            own = jnp.where(sec == layer, base, 0.0)
            if layer > 0:
                moved = dot((spread * gains[layer]).astype(BF16), downs[layer])
                along = jnp.sum(all_rows[layer].astype(F32) * spread, axis=-1, keepdims=True)
                inv = inv_rms[layer]
                later = inv * moved - (inv * inv * (1.0 / full_d)) * along * pre_act[layer]
                own = own + jnp.where(sec < layer, later, 0.0)
            terms.append(own)
        pay = jnp.concatenate(terms + [spread_up], axis=1).astype(BF16)
        result = run_tokens(pay.reshape(layers, part, 2 * layers * rank), consts, layers, full_d, 2 + it)
        result = result.reshape(tokens, 2 * layers * rank)

        back = [result[:, (layers + layer) * rank:(layers + layer + 1) * rank] for layer in range(layers)]
        pulls = []
        for layer in range(layers):
            inv = inv_rms[layer]
            pull = inv * inv * (1.0 / full_d) * jnp.sum(
                back[layer].astype(F32) * pre_act[layer], axis=-1, keepdims=True)
            pulls.append(jnp.where(sec < layer, pull, 0.0))
        acts = []
        for layer in range(layers):
            later = sum(pulls[layer + 1:], jnp.zeros((tokens, 1), F32))
            tan = result[:, layer * rank:(layer + 1) * rank].astype(F32)
            acts.append((tan - later * hidden[layer].astype(F32)).astype(BF16))
        cot = dot_t(jnp.concatenate(acts, axis=1), up_cat) - sum(pulls) * rows0.astype(F32)
        for layer in range(1, layers):
            moved = jnp.where(sec < layer, back[layer].astype(F32) * inv_rms[layer], 0.0).astype(BF16)
            cot = cot + dot_t(moved, downs[layer]) * gains[layer]
        grad_up = over_tokens(cot.astype(BF16), own_hidden)
        grad_down = over_tokens(own_normed, pick(back, sec))
        spread_shape = (YS, ZS, CS, own_rows, rank)
        part_a = grad_down.reshape(spread_shape)
        part_b = grad_up.reshape(spread_shape)
        if it == 0:
            gram_part = own_gram.reshape(YS, ZS, CS, layers * rank // (YS * ZS * CS), rank)
            part_b = jnp.concatenate([part_b, gram_part], axis=3)
        sum_a, sum_b = reduce_rows(part_a, part_b, 4 + it)
        if it == 0:
            hidden_gram = gather_rows(sum_b[own_rows:].reshape(2, -1, rank), 6)
            gram_rows_each = hidden_gram.shape[4]
            hidden_gram = hidden_gram.reshape(2, YS * ZS * CS, gram_rows_each, rank)
            hidden_gram = jnp.swapaxes(hidden_gram, 0, 1).reshape(layers, rank, rank)
            sum_b = sum_b[:own_rows]
        gram_parts = jnp.split(hidden_gram, layers, axis=0)
        high = hidden_gram.astype(BF16)
        rest = hidden_gram - high.astype(F32)
        middle = rest.astype(BF16)
        low = (rest - middle.astype(F32)).astype(BF16)
        for piece in (high, middle, low):
            sum_b = sum_b + lax.dot_general(
                up_shards, piece, (((0, 2), (0, 1)), ((), ())), preferred_element_type=F32)
        del gram_parts
        image = jnp.stack([sum_a, sum_b]) * (scales * norm_factor)

        count = base_count + it
        dots = jnp.sum(slots * image[None], axis=(1, 2, 3))
        square = jnp.sum(image * image)
        if it == 0:
            extra = gram_rows.reshape(-1)
        else:
            extra = jnp.sum(slots * slots[-1:], axis=(1, 2, 3))
        vec = jnp.concatenate([dots, square[None], extra])
        vec = jnp.pad(vec, (0, 128 - vec.shape[0]))
        total = sum_all(jnp.broadcast_to(vec[None], (8, 128)), layers, 7 + it)[0] * (1.0 / param_count)
        first = total[:count]
        image_square = total[count]
        if it == 0:
            gram = total[count + 1:count + 1 + count * count].reshape(count, count)
        else:
            row = total[count + 1:count + 1 + count]
            gram = jnp.concatenate([gram, row[None, :-1]], axis=0)
            gram = jnp.concatenate([gram, row[:, None]], axis=1)
        again = jnp.sum(gram * first[None, :], axis=1)
        coef = first + (first - again)
        gram_coef = jnp.sum(gram * coef[None, :], axis=1)
        length_square = image_square - 2.0 * jnp.sum(coef * first) + jnp.sum(coef * gram_coef)
        length = jnp.sqrt(jnp.maximum(length_square, 0.0) + VEC_EPS)
        cleaned = image - jnp.sum(coef.reshape(-1, 1, 1, 1) * slots, axis=0)
        fresh = cleaned / length
        new_vectors.append(fresh)
        hess.append(jnp.concatenate([coef, jnp.zeros((base_count + ITERS - count,), F32), length[None]]))
        if it + 1 < ITERS:
            slots = jnp.concatenate([slots, fresh[None]], axis=0)
            vector, up_shards = gather_vector((fresh * scales).astype(BF16), layers, 9)
            vector = vector.reshape(2, full_d, rank)
    return jnp.stack(new_vectors)[:, None], jnp.stack(hess)


def solution(mesh):
    return jax.shard_map(
        per_device,
        mesh=mesh,
        in_specs=(
            P(None, "replica", None),
            P("section", None, None),
            P("section", None, None),
            P("section", None),
            P(None, "section", None, "replica", None),
        ),
        out_specs=(P(None, "section", None, "replica", None), P()),
        check_vma=False,
    )
```

```python
import functools

import jax
import jax.numpy as jnp
from jax import lax
from jax.experimental import pallas as pl
from jax.experimental.pallas import tpu as pltpu
from jax.sharding import PartitionSpec as P

ITERS = 2
NORM_EPS = 1e-05
VEC_EPS = 1e-06

YS, ZS, CS = 4, 8, 2
HALF = ZS // 2
TILE = 512
MESH = pl.DeviceIdType.MESH
F32 = jnp.float32
BF16 = jnp.bfloat16
VMEM_BYTES = 56 * 1024 * 1024
Y_CHUNKS = 2


def dot(left, right):
    return jnp.dot(left, right, preferred_element_type=F32)


def dot_t(left, right):
    return lax.dot_general(left, right, (((1,), (1,)), ((), ())), preferred_element_type=F32)


def over_tokens(left, right):
    return lax.dot_general(left, right, (((0,), (0,)), ((), ())), preferred_element_type=F32)


def two_parts(wide):
    high = wide.astype(BF16)
    return high, (wide - high.astype(F32)).astype(BF16)


class Refs:
    def __init__(self, names, refs):
        self.__dict__.update(zip(names, refs, strict=True))


class Place:
    def __init__(self, layers):
        self.layers = layers
        self.sec, rep = lax.axis_index("section"), lax.axis_index("replica")
        self.core = lax.rem(rep, CS)
        self.zed = lax.rem(rep // CS, ZS)
        self.why = rep // (CS * ZS)
        self.inner, self.outer = ZS * CS, layers * YS
        self.here, self.there = self.zed * CS + self.core, self.sec * YS + self.why
        self.sibling = self.device(self.sec, self.why, self.zed, 1 - self.core)

    def device(self, sec, why, zed, core):
        return (sec, (why * ZS + zed) * CS + core)

    def y_at(self, step):
        return lax.rem(self.why + step + YS, YS)

    def z_at(self, step):
        return lax.rem(self.zed + step + ZS, ZS)

    def x(self, step):
        return self.device(lax.rem(self.sec + step, self.layers), self.why, self.zed, self.core)

    def y(self, step):
        return self.device(self.sec, self.y_at(step), self.zed, self.core)

    def z(self, step):
        return self.device(self.sec, self.why, self.z_at(step), self.core)

    def near(self, step):
        return (self.sec, self.why * self.inner + lax.rem(self.here + step, self.inner))

    def far(self, step):
        other = lax.rem(self.there + step, self.outer)
        return (other // YS, lax.rem(other, YS) * self.inner + self.here)

    def slot(self, layer):
        return lax.rem(layer - self.sec + self.layers, self.layers)


def greet(partners):
    barrier = pltpu.get_barrier_semaphore()
    for partner in partners:
        pl.semaphore_signal(barrier, inc=1, device_id=partner, device_id_type=MESH)
    pl.semaphore_wait(barrier, len(partners))


def remote(src, dst, send_sem, recv_sem, partner):
    return pltpu.make_async_remote_copy(
        src_ref=src,
        dst_ref=dst,
        send_sem=send_sem,
        recv_sem=recv_sem,
        device_id=partner,
        device_id_type=MESH,
    )


def exchange(sends, count, partner, source, landing, send, recv):
    copies = []
    for step in range(1, count):
        copy = remote(source(step), landing(step), send.at[step - 1], recv.at[step - 1], partner(step))
        copy.start()
        copies.append(copy)
    sends += copies
    return copies


def arrived(ref, send, recv, at, partner):
    remote(ref, ref, send.at[at], recv.at[at], partner).wait_recv()


def drain(sends):
    for copy in sends:
        copy.wait_send()
    sends.clear()


def merged(*threads):
    threads = list(threads)
    while threads:
        for thread in list(threads):
            try:
                next(thread)
            except StopIteration:
                threads.remove(thread)
                continue
            yield


def finish(thread):
    for _ in thread:
        pass


GATHER_KINDS = 12


def gather_sems(blocks):
    first = blocks // 2
    dma = pltpu.SemaphoreType.DMA
    ring = (2 * ZS, first)
    return [dma((YS - 1,)), dma((YS - 1,)), dma(ring), dma(ring), dma(ring), dma(ring),
            dma((2 * ZS,)), dma((2 * ZS,)), dma((YS,)), dma((YS,)), dma((YS,)), dma((YS,))]


def ring_steps():
    return [(step, way) for step in range(1, HALF + 1) for way in (1, -1) if way > 0 or step < HALF]


def gather_first(out, blocks, at, sems, sends):
    ysend, yrecv, zsend, zrecv, csend, crecv = sems
    mine = out.at[pl.ds(blocks[0], len(blocks)), at.why, at.zed, at.core]
    exchange(sends, YS, at.y, lambda step: mine, lambda step: mine, ysend, yrecv)

    def bundle(chunk, z, core):
        return out.at[blocks[chunk], :, z, core]

    def index(step, way):
        return 2 * step + (way > 0)

    def send(step, way, chunk):
        view = bundle(chunk, at.z_at(-way * (step - 1)), at.core)
        copy = remote(view, view, zsend.at[index(step, way), chunk], zrecv.at[index(step, way), chunk],
                      at.z(way))
        copy.start()
        sends.append(copy)

    def hand_on(step, way, chunk):
        view = bundle(chunk, at.z_at(-way * step), at.core)
        copy = remote(view, view, csend.at[index(step, way), chunk], crecv.at[index(step, way), chunk],
                      at.sibling)
        copy.start()
        sends.append(copy)

    yield
    for step in range(1, YS):
        block = out.at[pl.ds(blocks[0], len(blocks)), at.y_at(-step), at.zed, at.core]
        arrived(block, ysend, yrecv, step - 1, at.sibling)
    for chunk in range(len(blocks)):
        send(1, 1, chunk)
        send(1, -1, chunk)
    for chunk in range(len(blocks)):
        hand_on(0, 1, chunk)
    steps = ring_steps()
    for step in range(1, HALF + 1):
        for chunk in range(len(blocks)):
            yield
            for way in (1, -1):
                if (step, way) not in steps:
                    continue
                view = bundle(chunk, at.z_at(-way * step), at.core)
                remote(view, view, zsend.at[index(step, way), chunk], zrecv.at[index(step, way), chunk],
                       at.sibling).wait_recv()
                if (step + 1, way) in steps:
                    send(step + 1, way, chunk)
                hand_on(step, way, chunk)
    for step, way in [(0, 1)] + steps:
        yield
        for chunk in range(len(blocks)):
            view = bundle(chunk, at.z_at(-way * step), 1 - at.core)
            remote(view, view, csend.at[index(step, way), chunk], crecv.at[index(step, way), chunk],
                   at.sibling).wait_recv()


def gather_second(out, blocks, at, sems, sends):
    zsend, zrecv, ysend, yrecv, csend, crecv = sems
    span = pl.ds(blocks[0], len(blocks))

    def view(z):
        return out.at[span, at.why, z, at.core]

    def index(step, way):
        return 2 * step + (way > 0)

    def send(step, way):
        block = view(at.z_at(-way * (step - 1)))
        copy = remote(block, block, zsend.at[index(step, way)], zrecv.at[index(step, way)], at.z(way))
        copy.start()
        sends.append(copy)

    def bundle(step, core, part=None):
        zeds = pl.ds(0, ZS) if part is None else pl.ds(part * HALF, HALF)
        return out.at[span, at.y_at(step), zeds, core]

    def along(ref, idx, way):
        copy = remote(ref, ref, ysend.at[idx], yrecv.at[idx], at.y(way))
        copy.start()
        sends.append(copy)

    def hand_on(step, idx):
        ref = bundle(step, at.core)
        copy = remote(ref, ref, csend.at[idx], crecv.at[idx], at.sibling)
        copy.start()
        sends.append(copy)

    send(1, 1)
    send(1, -1)
    steps = ring_steps()
    for step in range(1, HALF + 1):
        yield
        for way in (1, -1):
            if (step, way) not in steps:
                continue
            block = view(at.z_at(-way * step))
            remote(block, block, zsend.at[index(step, way)], zrecv.at[index(step, way)],
                   at.sibling).wait_recv()
            if (step + 1, way) in steps:
                send(step + 1, way)
    along(bundle(0, at.core), 0, 1)
    along(bundle(0, at.core), 1, -1)
    hand_on(0, 0)
    yield
    arrived(bundle(-1, at.core), ysend, yrecv, 0, at.sibling)
    along(bundle(-1, at.core, 0), 2, 1)
    arrived(bundle(1, at.core), ysend, yrecv, 1, at.sibling)
    along(bundle(1, at.core, 1), 3, -1)
    hand_on(-1, 1)
    hand_on(1, 2)
    yield
    arrived(bundle(2, at.core, 0), ysend, yrecv, 2, at.sibling)
    arrived(bundle(2, at.core, 1), ysend, yrecv, 3, at.sibling)
    hand_on(2, 3)
    for idx, step in enumerate((0, -1, 1, 2)):
        yield
        arrived(bundle(step, 1 - at.core), csend, crecv, idx, at.sibling)


def gather(out, start, count, at, sems, sends):
    half = count // 2
    first = list(range(start, start + half))
    second = list(range(start + half, start + count))
    return merged(gather_second(out, second, at, sems[6:], sends),
                  gather_first(out, first, at, sems[:6], sends))


def row_block(ref, block, idx):
    per = TILE // (CS * 64)
    wide = ref[block, idx // (ZS // per), pl.ds((idx % (ZS // per)) * per, per)]
    return wide.reshape(TILE, 128)


def tiles(full_d, body):
    def step(idx, carry):
        body(idx, pl.ds(pl.multiple_of(idx * TILE, TILE), TILE))
        return carry
    lax.fori_loop(0, full_d // TILE, step, 0)


def lane_sums(wide):
    return sum(wide[:, start:start + 128] for start in range(0, TILE, 128))


def primal(ref, at, full_d, between):
    layers, sec = at.layers, at.sec
    tokens = ref.rows.shape[0]
    part = tokens // layers
    acc, along = ref.acc, ref.along
    mine = pl.ds(pl.multiple_of(sec * part, part), part)
    along[0] = jnp.zeros((tokens, 128), F32)

    def rows_of(layer, where, cols):
        return ref.rows[where, cols] if layer == 0 else ref.every_row[layer - 1, where, cols]

    everywhere = slice(None)

    def square(idx, cols):
        wide = ref.rows[:, cols].astype(F32)
        along[0] += lane_sums(wide * wide)
    tiles(full_d, square)
    for layer in range(layers):
        down, up = 2 * at.slot(layer), 2 * at.slot(layer) + 1
        mean = jnp.sum(along[0], axis=-1, keepdims=True) * (1.0 / full_d)
        inv = lax.rsqrt(mean + NORM_EPS)
        acc[0] = jnp.zeros((tokens, 128), F32)

        def project(idx, cols):
            gain = ref.gains[at.slot(layer), :, cols]
            piece = (rows_of(layer, everywhere, cols).astype(F32) * inv * gain).astype(BF16)

            @pl.when(sec == layer)
            def _():
                ref.normed[:, cols] = piece
            acc[0] += dot(piece, row_block(ref.weights, down, idx))
        tiles(full_d, project)
        between()
        pre = acc[0]
        sig = jax.nn.sigmoid(pre)
        act = (pre * sig).astype(BF16)
        ref.hidden[:, layer * 128:(layer + 1) * 128] = act

        @pl.when(sec == layer)
        def _():
            ref.own_hidden[...] = act
        ref.pre_act[layer] = pre
        ref.slope[layer] = sig + pre * sig * (1.0 - sig)
        ref.inv_rms[layer] = jnp.broadcast_to(inv, (tokens, 128))
        along[0] = jnp.zeros((tokens, 128), F32)
        if layer + 1 < layers:
            def forward(idx, cols):
                wide = rows_of(layer, everywhere, cols).astype(F32)
                wide = wide + dot_t(act, row_block(ref.weights, up, idx))
                rounded = wide.astype(BF16)
                ref.every_row[layer, :, cols] = rounded
                again = rounded.astype(F32)
                along[0] += lane_sums(again * again)
            tiles(full_d, forward)
            between()
    ref.uu[...] = jnp.zeros_like(ref.uu)
    ref.ud[...] = jnp.zeros_like(ref.ud)
    ref.row_up[...] = jnp.zeros_like(ref.row_up)

    def grams(idx, cols):
        ups = [row_block(ref.weights, 2 * at.slot(layer) + 1, idx) for layer in range(layers)]
        every = jnp.concatenate(ups, axis=1)
        turned = every.T
        ref.uu[...] += dot(turned, every)
        pair_at = 0
        for layer in range(1, layers):
            width = layer * 128
            gain = ref.gains[at.slot(layer), :, cols]
            high, low = two_parts(turned[:width].astype(F32) * gain)
            down = row_block(ref.weights, 2 * at.slot(layer), idx)
            pair = dot(high, down) + dot(low, down)
            block = dot(rows_of(layer, mine, cols), every[:, :width])
            for k in range(layer):
                ref.ud[pair_at] += pair[k * 128:(k + 1) * 128]
                ref.row_up[pair_at] += block[:, k * 128:(k + 1) * 128]
                pair_at += 1
    tiles(full_d, grams)
    between()
    ref.uu_high[...], ref.uu_low[...] = two_parts(ref.uu[...])
    ref.ud_high[...], ref.ud_low[...] = two_parts(ref.ud[...])
    ref.gram[...] = over_tokens(ref.hidden[...], ref.own_hidden[...])


def recurrence(tan_base, back_base, pre_act, slope, inv_rms, row_up, up_up, up_down, full_d):
    layers = len(tan_base)
    tan_act = []
    for layer in range(layers):
        tan_pre = tan_base[layer]
        if layer > 0:
            moved = sum(dot(tan_act[k], up_down[k][layer][0]) + dot(tan_act[k], up_down[k][layer][1])
                        for k in range(layer))
            along = sum(jnp.sum(tan_act[k].astype(F32) * row_up[layer][k], axis=-1, keepdims=True)
                        for k in range(layer))
            inv = inv_rms[layer]
            tan_pre = tan_pre + inv * moved - (inv * inv * (1.0 / full_d)) * along * pre_act[layer]
        tan_act.append((tan_pre * slope[layer]).astype(BF16))
    every = jnp.concatenate(tan_act, axis=1)
    back_all = dot(every, up_up[0]) + dot(every, up_up[1])
    back_pre, moved_back, pull = {}, {}, {}
    for layer in reversed(range(layers)):
        back_act = back_base[layer] + back_all[:, layer * 128:(layer + 1) * 128]
        for k in range(layer + 1, layers):
            back_act = back_act + dot_t(moved_back[k], up_down[layer][k][0])
            back_act = back_act + dot_t(moved_back[k], up_down[layer][k][1])
            back_act = back_act - pull[k] * row_up[k][layer]
        piece = (back_act * slope[layer]).astype(BF16)
        wide = piece.astype(F32)
        inv = inv_rms[layer]
        back_pre[layer] = piece
        moved_back[layer] = (wide * inv).astype(BF16)
        pull[layer] = inv * inv * (1.0 / full_d) * jnp.sum(wide * pre_act[layer], axis=-1, keepdims=True)
    return tan_act + [back_pre[layer] for layer in range(layers)]


def token_terms(ref, at, full_d):
    layers, sec = at.layers, at.sec
    acc, along = ref.acc, ref.along
    acc[...] = jnp.zeros_like(acc)
    along[...] = jnp.zeros_like(along)
    own_hidden = ref.own_hidden[...]
    part = own_hidden.shape[0] // layers

    def body(idx, cols):
        acc[0] += dot(ref.normed[:, cols], row_block(ref.vector, 0, idx))
        spread = dot_t(own_hidden, row_block(ref.vector, 1, idx))
        rounded = spread.astype(BF16)
        for layer in range(layers):
            acc[layers + layer] += dot(rounded, row_block(ref.weights, 2 * at.slot(layer) + 1, idx))
        for layer in range(1, layers):
            scaled = (spread * ref.gains[at.slot(layer), :, cols]).astype(BF16)
            acc[layer] += dot(scaled, row_block(ref.weights, 2 * at.slot(layer), idx))
            along[layer] += lane_sums(ref.every_row[layer - 1, :, cols].astype(F32) * spread)
    tiles(full_d, body)
    base = acc[0]

    def put(block, value):
        value = value.astype(BF16)
        for quarter in range(layers):
            ref.pay[quarter, :, block * 128:(block + 1) * 128] = value[quarter * part:(quarter + 1) * part]
    for layer in range(layers):
        own = jnp.where(sec == layer, base, 0.0)
        if layer > 0:
            inv = ref.inv_rms[layer]
            reach = jnp.sum(along[layer], axis=-1, keepdims=True)
            later = inv * acc[layer] - (inv * inv * (1.0 / full_d)) * reach * ref.pre_act[layer]
            own = own + jnp.where(sec < layer, later, 0.0)
        put(layer, own)
        put(layers + layer, acc[layers + layer])


def gradient_terms(ref, at, full_d):
    layers, sec = at.layers, at.sec
    res = ref.result
    part = res.shape[1]
    tokens = part * layers

    def column(block):
        return jnp.concatenate([res[q, :, block * 128:(block + 1) * 128] for q in range(layers)], axis=0)
    back = [column(layers + layer) for layer in range(layers)]
    pulls, moved = [], []
    for layer in range(layers):
        inv = ref.inv_rms[layer]
        wide = back[layer].astype(F32)
        pull = inv * inv * (1.0 / full_d) * jnp.sum(wide * ref.pre_act[layer], axis=-1, keepdims=True)
        pulls.append(jnp.where(sec < layer, pull, 0.0))
        moved.append(jnp.where(sec < layer, wide * inv, 0.0).astype(BF16))
    acts = []
    later = jnp.zeros((tokens, 128), F32)
    for layer in reversed(range(layers)):
        old = ref.hidden[:, layer * 128:(layer + 1) * 128].astype(F32)
        acts.insert(0, (column(layer).astype(F32) - later * old).astype(BF16))
        later = later + pulls[layer]
    total = later[:, :1]
    own_back = back[0]
    for layer in range(1, layers):
        own_back = jnp.where(sec == layer, back[layer], own_back)
    own_hidden = ref.own_hidden[...]
    per = TILE // (CS * 64)

    def body(idx, cols):
        cot = -total * ref.rows[:, cols].astype(F32)
        for layer in range(layers):
            cot = cot + dot_t(acts[layer], row_block(ref.weights, 2 * at.slot(layer) + 1, idx))
        for layer in range(1, layers):
            cot = cot + (dot_t(moved[layer], row_block(ref.weights, 2 * at.slot(layer), idx))
                         * ref.gains[at.slot(layer), :, cols])
        where = (idx // (ZS // per), pl.ds((idx % (ZS // per)) * per, per))
        ref.part_b[where] = over_tokens(cot.astype(BF16), own_hidden).reshape(per, CS, 64, 128)
        ref.part_a[where] = over_tokens(ref.normed[:, cols], own_back).reshape(per, CS, 64, 128)
        for copy in swap_copies(ref, at, idx):
            copy.start()
    tiles(full_d, body)


def swap_copies(ref, at, idx):
    per = TILE // (CS * 64)
    where = (idx // (ZS // per), pl.ds((idx % (ZS // per)) * per, per))
    other = where + (1 - at.core,)
    return (
        remote(ref.part_b.at[other], ref.swap_b.at[where], ref.swap_send.at[0, idx], ref.swap_recv.at[0, idx],
               at.sibling),
        remote(ref.part_a.at[other], ref.swap_a.at[where], ref.swap_send.at[1, idx], ref.swap_recv.at[1, idx],
               at.sibling),
    )


def scatter_first(ref, at, sends, done):
    left_in, right_in, y_in = ref.left_in, ref.right_in, ref.y_a
    size = YS // Y_CHUNKS

    def chunk_of(chunk):
        return pl.ds(chunk * size, size)

    def chip_sum(z, chunk):
        span = chunk_of(chunk)
        return ref.swap_a[span, z] + ref.part_a[span, z, at.core]

    def left(step, chunk):
        z = at.z_at(step - HALF - 1)
        return remote(ref.out_a.at[chunk_of(chunk), z], left_in.at[step - 1, chunk_of(chunk)],
                      ref.ls.at[step - 1, chunk], ref.lr.at[step - 1, chunk], at.z(-1))

    def right(step, chunk):
        z = at.z_at(HALF - step)
        return remote(ref.out_a.at[chunk_of(chunk), z], right_in.at[step - 1, chunk_of(chunk)],
                      ref.rs.at[step - 1, chunk], ref.rr.at[step - 1, chunk], at.z(1))

    def go(copy):
        copy.start()
        sends.append(copy)

    for step in range(1, HALF + 1):
        for chunk in range(Y_CHUNKS):
            if step > 1:
                yield
            span = chunk_of(chunk)
            z = at.z_at(step - HALF - 1)
            value = chip_sum(z, chunk)
            if step > 1:
                left(step - 1, chunk).wait_recv()
                value = value + left_in[step - 2, span]
            ref.out_a[span, z] = value
            go(left(step, chunk))
            if step < HALF:
                z = at.z_at(HALF - step)
                value = chip_sum(z, chunk)
                if step > 1:
                    right(step - 1, chunk).wait_recv()
                    value = value + right_in[step - 2, span]
                ref.out_a[span, z] = value
                go(right(step, chunk))
    yield
    for chunk in range(Y_CHUNKS):
        span = chunk_of(chunk)
        value = chip_sum(at.zed, chunk)
        right(HALF - 1, chunk).wait_recv()
        value = value + right_in[HALF - 2, span]
        left(HALF, chunk).wait_recv()
        ref.out_a[span, at.zed] = value + left_in[HALF - 1, span]

    copies = exchange(sends, YS, at.y, lambda step: ref.out_a.at[at.y_at(step), at.zed],
                      lambda step: y_in.at[step - 1], ref.yas, ref.yar)
    yield
    value = ref.out_a[at.why, at.zed]
    for step, copy in enumerate(copies):
        copy.wait_recv()
        value = value + y_in[step]
    done.append(value)


def scatter_second(ref, at, sends, done):
    halves = (pl.ds(0, HALF), pl.ds(HALF, HALF))
    out = ref.out_b

    def chip_sum(step, half):
        y = at.y_at(step)
        return ref.swap_b[y, halves[half]] + ref.part_b[y, halves[half], at.core]

    def go(src, dst, idx, way):
        copy = remote(src, dst, ref.ybs.at[idx], ref.ybr.at[idx], at.y(way))
        copy.start()
        sends.append(copy)

    def took(dst, idx):
        arrived(dst, ref.ybs, ref.ybr, idx, at.sibling)

    def view(step, half):
        return out.at[at.y_at(step), halves[half]]

    out[at.y_at(2), halves[0]] = chip_sum(2, 0)
    go(view(2, 0), ref.chain.at[0], 0, 1)
    out[at.y_at(2), halves[1]] = chip_sum(2, 1)
    go(view(2, 1), ref.chain.at[1], 1, -1)
    out[at.y_at(1), halves[1]] = chip_sum(1, 1)
    go(view(1, 1), ref.from_low.at[halves[1]], 2, 1)
    out[at.y_at(-1), halves[0]] = chip_sum(-1, 0)
    go(view(-1, 0), ref.from_high.at[halves[0]], 3, -1)
    yield
    took(ref.chain.at[0], 0)
    out[at.y_at(1), halves[0]] = chip_sum(1, 0) + ref.chain[0]
    go(view(1, 0), ref.from_low.at[halves[0]], 4, 1)
    took(ref.chain.at[1], 1)
    out[at.y_at(-1), halves[1]] = chip_sum(-1, 1) + ref.chain[1]
    go(view(-1, 1), ref.from_high.at[halves[1]], 5, -1)
    yield
    yield
    yield
    took(ref.from_low.at[halves[1]], 2)
    took(ref.from_high.at[halves[0]], 3)
    took(ref.from_low.at[halves[0]], 4)
    took(ref.from_high.at[halves[1]], 5)
    for half in range(2):
        out[at.why, halves[half]] = (
            chip_sum(0, half) + ref.from_low[halves[half]] + ref.from_high[halves[half]])
    copies = exchange(sends, ZS, at.z, lambda step: out.at[at.why, at.z_at(step)],
                      lambda step: ref.z_b.at[step - 1], ref.zbs, ref.zbr)
    yield
    yield
    yield
    value = out[at.why, at.zed]
    for step, copy in enumerate(copies):
        copy.wait_recv()
        value = value + ref.z_b[step]
    done.append(value)


def scatter_sum(ref, at, full_d, sends):
    for idx in range(full_d // TILE):
        for copy in swap_copies(ref, at, idx):
            copy.wait_recv()
            sends.append(copy)
    done_a, done_b = [], []
    finish(merged(scatter_second(ref, at, sends, done_b), scatter_first(ref, at, sends, done_a)))
    return done_a[0], done_b[0]


def gram_steps(ref, at, sends):
    gram, whole = ref.gram, ref.hidden_gram
    piece = gram.shape[0] // at.inner
    small = piece // YS

    def rows(index, size):
        return pl.ds(pl.multiple_of(index * size, size), size)

    copies = exchange(sends, at.inner, at.near,
                      lambda step: gram.at[rows(lax.rem(at.here + step, at.inner), piece)],
                      lambda step: ref.gram_in.at[step - 1], ref.g1s, ref.g1r)
    yield
    value = gram[rows(at.here, piece), :]
    for step, copy in enumerate(copies):
        copy.wait_recv()
        value = value + ref.gram_in[step]
    ref.gram_sum[...] = value
    copies = exchange(sends, YS, at.y, lambda step: ref.gram_sum.at[rows(at.y_at(step), small)],
                      lambda step: ref.gram_in2.at[step - 1], ref.g2s, ref.g2r)
    yield
    own = rows(at.why, small)
    value = ref.gram_sum[own, :]
    for step, copy in enumerate(copies):
        copy.wait_recv()
        value = value + ref.gram_in2[step]
    ref.gram_out[own, :] = value
    exchange(sends, YS, at.y, lambda step: ref.gram_out.at[own], lambda step: ref.gram_out.at[own],
             ref.g3s, ref.g3r)
    yield
    for step in range(1, YS):
        arrived(ref.gram_out.at[rows(at.y_at(-step), small)], ref.g3s, ref.g3r, step - 1, at.sibling)
    mine = rows(at.here, piece)
    whole[mine, :] = ref.gram_out[...]
    exchange(sends, at.inner, at.near, lambda step: ref.gram_out, lambda step: whole.at[mine],
             ref.g4s, ref.g4r)
    yield
    for step in range(1, at.inner):
        source = rows(lax.rem(at.here + at.inner - step, at.inner), piece)
        arrived(whole.at[source], ref.g4s, ref.g4r, step - 1, at.sibling)


def sum_all(ref, at, line, sends):
    vec, near, far, half_sum = ref.vec, ref.near, ref.far, ref.half_sum
    vec[...] = jnp.broadcast_to(line, vec.shape)
    exchange(sends, at.inner, at.near, lambda step: vec, lambda step: near.at[at.here], ref.ns, ref.nr)
    near[at.here] = vec[...]
    for step in range(1, at.inner):
        slot = near.at[lax.rem(at.here + at.inner - step, at.inner)]
        arrived(slot, ref.ns, ref.nr, step - 1, at.sibling)
    half_sum[...] = jnp.sum(near[...], axis=0)
    exchange(sends, at.outer, at.far, lambda step: half_sum, lambda step: far.at[at.there], ref.fs, ref.fr)
    far[at.there] = half_sum[...]
    for step in range(1, at.outer):
        slot = far.at[lax.rem(at.there + at.outer - step, at.outer)]
        arrived(slot, ref.fs, ref.fr, step - 1, at.sibling)
    return jnp.sum(far[...], axis=0)[:1]


def put_vector(ref, at, down_rows, up_rows, full_d, rank, sends):
    ref.shard[0] = (down_rows * (full_d ** -0.5)).astype(BF16)
    ref.shard[1] = (up_rows * (rank ** -0.5)).astype(BF16)
    ref.vector[:, at.why, at.zed, at.core] = ref.shard[...]
    ref.ups[0] = ref.shard[1]
    exchange(sends, at.layers, at.x, lambda step: ref.shard.at[1],
             lambda step: ref.ups.at[at.layers - step], ref.x3s, ref.x3r)


def ups_arrived(ref, at):
    for step in range(1, at.layers):
        arrived(ref.ups.at[at.layers - step], ref.x3s, ref.x3r, step - 1, at.sibling)


def curvature(ref, at, full_d, sends, between):
    layers, sec = at.layers, at.sec
    token_terms(ref, at, full_d)
    pay = ref.pay
    copies = exchange(sends, layers, at.x, lambda step: pay.at[lax.rem(sec + step, layers)],
                      lambda step: ref.pay_in.at[step - 1], ref.x1s, ref.x1r)
    total = pay[sec].astype(F32)
    for step, copy in enumerate(copies):
        copy.wait_recv()
        total = total + ref.pay_in[step].astype(F32)
    between()
    row_up = {}
    up_down = {k: {} for k in range(layers)}
    idx = 0
    for layer in range(layers):
        for k in range(layer):
            row_up.setdefault(layer, {})[k] = ref.row_up[idx]
            up_down[k][layer] = (ref.ud_high[idx], ref.ud_low[idx])
            idx += 1
    part = pay.shape[1]
    mine = pl.ds(pl.multiple_of(sec * part, part), part)
    pieces = recurrence(
        [total[:, start * 128:(start + 1) * 128] for start in range(layers)],
        [total[:, start * 128:(start + 1) * 128] for start in range(layers, 2 * layers)],
        [ref.pre_act[layer, mine, :] for layer in range(layers)],
        [ref.slope[layer, mine, :] for layer in range(layers)],
        [ref.inv_rms[layer, mine, :] for layer in range(layers)],
        row_up, (ref.uu_high[...], ref.uu_low[...]), up_down, full_d)
    result = ref.result
    result[sec] = jnp.concatenate(pieces, axis=1)
    own = result.at[sec]
    exchange(sends, layers, at.x, lambda step: own, lambda step: own, ref.x2s, ref.x2r)
    between()
    for step in range(1, layers):
        arrived(result.at[lax.rem(sec + layers - step, layers)], ref.x2s, ref.x2r, step - 1, at.sibling)
    between()
    gradient_terms(ref, at, full_d)
    return scatter_sum(ref, at, full_d, sends)


def main_kernel(cfg, names, *refs):
    layers, tokens_all, base_count = cfg
    ref = Refs(names, refs)
    at = Place(layers)
    full_d, rank = ref.rows.shape[1], ref.down.shape[-1]
    sends = []
    lane = lax.broadcasted_iota(jnp.int32, (1, 128), 1)
    copies = [pltpu.make_async_copy(ref.down, ref.weights.at[0], ref.local.at[0]),
              pltpu.make_async_copy(ref.up, ref.weights.at[1], ref.local.at[1])]
    for copy in copies:
        copy.start()
    ref.gains[0] = ref.gain[...]
    greet([at.near(step) for step in range(1, at.inner)] + [at.far(step) for step in range(1, at.outer)])

    for block, source in enumerate((ref.down, ref.up)):
        row = source.at[at.why, at.zed, at.core]
        exchange(sends, layers, at.x, lambda step: row,
                 lambda step: ref.weights.at[2 * (layers - step) + block, at.why, at.zed, at.core],
                 ref.xws.at[block], ref.xwr.at[block])
    exchange(sends, layers, at.x, lambda step: ref.gain, lambda step: ref.gains.at[layers - step],
             ref.xgs, ref.xgr)
    put_vector(ref, at, ref.basis[base_count - 1, 0], ref.basis[base_count - 1, 1], full_d, rank, sends)
    for step in range(1, layers):
        for block in range(2):
            arrived(ref.weights.at[2 * (layers - step) + block, at.why, at.zed, at.core],
                    ref.xws.at[block], ref.xwr.at[block], step - 1, at.sibling)
    sems = [ref.__dict__[key] for key in range(2 * GATHER_KINDS)]
    finish(gather(ref.weights, 2, 2 * layers - 2, at, sems[:GATHER_KINDS], sends))
    for step in range(1, layers):
        arrived(ref.gains.at[layers - step], ref.xgs, ref.xgr, step - 1, at.sibling)
    for copy in copies:
        copy.wait()
    moving = gather(ref.vector, 0, 2, at, sems[GATHER_KINDS:], sends)

    def move():
        next(moving, None)
        next(moving, None)
    move()
    primal(ref, at, full_d, move)
    finish(moving)
    ups_arrived(ref, at)
    drain(sends)

    norm = 1.0 / tokens_all
    scales = (full_d ** -0.5, rank ** -0.5)
    held = [(ref.basis[k, 0], ref.basis[k, 1]) for k in range(base_count)]
    gram_slots = {}

    def gram_at(k, j):
        return gram_slots[max(k, j), min(k, j)]

    def inner_sum(left, right):
        both = left[0] * right[0] + left[1] * right[1]
        return jnp.sum(jnp.sum(both, axis=0, keepdims=True), axis=1, keepdims=True)

    for it in range(ITERS):
        count = base_count + it
        summing = gram_steps(ref, at, sends) if it == 0 else iter(())
        next(summing, None)
        sum_a, sum_b = curvature(ref, at, full_d, sends, lambda: next(summing, None))
        finish(summing)
        for layer in range(layers):
            wide = ref.hidden_gram[layer * rank:(layer + 1) * rank, :]
            high = wide.astype(BF16)
            rest = wide - high.astype(F32)
            middle, low = two_parts(rest)
            ups = ref.ups[at.slot(layer)]
            sum_b = sum_b + dot(ups, high) + dot(ups, middle) + dot(ups, low)
        image = [sum_a * (scales[0] * norm), sum_b * (scales[1] * norm)]

        pairs = [(k, j) for k in range(count) for j in range(k + 1) if (k, j) not in gram_slots]
        values = [inner_sum(item, image) for item in held] + [inner_sum(image, image)]
        values += [inner_sum(held[k], held[j]) for k, j in pairs]
        line = jnp.zeros((1, 128), F32)
        for place, value in enumerate(values):
            line = jnp.where(lane == place, value, line)
        line = sum_all(ref, at, line, sends) * (1.0 / (layers * 2 * full_d * rank))
        totals = [jnp.sum(jnp.where(lane == place, line, 0.0), axis=1, keepdims=True)
                  for place in range(len(values))]
        first_coef, image_square = totals[:count], totals[count]
        gram_slots.update(zip(pairs, totals[count + 1:]))
        coef, length_square = [], image_square
        for k in range(count):
            again = sum(gram_at(k, j) * first_coef[j] for j in range(count))
            coef.append(first_coef[k] + (first_coef[k] - again))
        for k in range(count):
            mixed = sum(gram_at(k, j) * coef[j] for j in range(count))
            length_square = length_square + coef[k] * (mixed - 2.0 * first_coef[k])
        length = jnp.sqrt(jnp.maximum(length_square, 0.0) + VEC_EPS)
        fresh = []
        for block in range(2):
            clean = image[block]
            for k in range(count):
                clean = clean - coef[k] * held[k][block]
            fresh.append(clean / length)
            ref.fresh[it, block] = fresh[block]
        line = jnp.zeros((1, 128), F32)
        for k in range(count):
            line = jnp.where(lane == k, coef[k], line)
        line = jnp.where(lane == base_count + ITERS, length, line)
        ref.hess[it] = jnp.broadcast_to(line, (8, 128))
        drain(sends)
        if it + 1 < ITERS:
            held.append((ref.fresh[it, 0], ref.fresh[it, 1]))
            put_vector(ref, at, fresh[0], fresh[1], full_d, rank, sends)
            finish(gather(ref.vector, 0, 2, at, sems[GATHER_KINDS:], sends))
            ups_arrived(ref, at)
            drain(sends)


def per_device(hidden_in, down_weight, up_weight, norm_gain, krylov_basis):
    layers = lax.axis_size("section")
    micro, tok, full_d = hidden_in.shape
    rank = down_weight.shape[2]
    tokens = micro * tok
    part = tokens // layers
    basis = krylov_basis[:, 0]
    base_count, _, rows, _ = basis.shape
    split = (YS, ZS, CS, rows, rank)
    vmem = pl.BlockSpec(memory_space=pltpu.VMEM)
    hbm = pl.BlockSpec(memory_space=pl.ANY)
    dma = pltpu.SemaphoreType.DMA
    inner, outer = ZS * CS, layers * YS
    pairs = layers * (layers - 1) // 2
    wide = layers * rank
    piece = wide // inner

    inputs = dict(
        rows=hidden_in.reshape(tokens, full_d),
        down=down_weight[0].reshape(split),
        up=up_weight[0].reshape(split),
        gain=norm_gain,
        basis=basis,
    )
    outputs = dict(
        fresh=jax.ShapeDtypeStruct((ITERS, 2, rows, rank), F32),
        hess=jax.ShapeDtypeStruct((ITERS, 8, 128), F32),
    )
    scratch = dict(
        weights=pltpu.VMEM((2 * layers,) + split, BF16),
        vector=pltpu.VMEM((2,) + split, BF16),
        gains=pltpu.VMEM((layers, 1, full_d), F32),
        ups=pltpu.VMEM((layers, rows, rank), BF16),
        shard=pltpu.VMEM((2, rows, rank), BF16),
        every_row=pltpu.VMEM((layers - 1, tokens, full_d), BF16),
        normed=pltpu.VMEM((tokens, full_d), BF16),
        hidden=pltpu.VMEM((tokens, wide), BF16),
        own_hidden=pltpu.VMEM((tokens, rank), BF16),
        pre_act=pltpu.VMEM((layers, tokens, rank), F32),
        slope=pltpu.VMEM((layers, tokens, rank), F32),
        inv_rms=pltpu.VMEM((layers, tokens, 128), F32),
        row_up=pltpu.VMEM((pairs, part, rank), F32),
        uu=pltpu.VMEM((wide, wide), F32),
        ud=pltpu.VMEM((pairs, rank, rank), F32),
        uu_high=pltpu.VMEM((wide, wide), BF16),
        uu_low=pltpu.VMEM((wide, wide), BF16),
        ud_high=pltpu.VMEM((pairs, rank, rank), BF16),
        ud_low=pltpu.VMEM((pairs, rank, rank), BF16),
        gram=pltpu.VMEM((wide, rank), F32),
        hidden_gram=pltpu.VMEM((wide, rank), F32),
        gram_in=pltpu.VMEM((inner - 1, piece, rank), F32),
        gram_sum=pltpu.VMEM((piece, rank), F32),
        gram_in2=pltpu.VMEM((YS - 1, piece // YS, rank), F32),
        gram_out=pltpu.VMEM((piece, rank), F32),
        acc=pltpu.VMEM((2 * layers, tokens, rank), F32),
        along=pltpu.VMEM((layers, tokens, 128), F32),
        pay=pltpu.VMEM((layers, part, 2 * wide), BF16),
        pay_in=pltpu.VMEM((layers - 1, part, 2 * wide), BF16),
        result=pltpu.VMEM((layers, part, 2 * wide), BF16),
        part_a=pltpu.VMEM(split, F32),
        part_b=pltpu.VMEM(split, F32),
        swap_a=pltpu.VMEM((YS, ZS, rows, rank), F32),
        swap_b=pltpu.VMEM((YS, ZS, rows, rank), F32),
        out_a=pltpu.VMEM((YS, ZS, rows, rank), F32),
        out_b=pltpu.VMEM((YS, ZS, rows, rank), F32),
        left_in=pltpu.VMEM((HALF, YS, rows, rank), F32),
        right_in=pltpu.VMEM((HALF - 1, YS, rows, rank), F32),
        y_a=pltpu.VMEM((YS - 1, rows, rank), F32),
        chain=pltpu.VMEM((2, HALF, rows, rank), F32),
        from_low=pltpu.VMEM((ZS, rows, rank), F32),
        from_high=pltpu.VMEM((ZS, rows, rank), F32),
        z_b=pltpu.VMEM((ZS - 1, rows, rank), F32),
        vec=pltpu.VMEM((8, 128), F32),
        near=pltpu.VMEM((inner, 8, 128), F32),
        far=pltpu.VMEM((outer, 8, 128), F32),
        half_sum=pltpu.VMEM((8, 128), F32),
        local=dma((2,)),
        xws=dma((2, layers - 1)), xwr=dma((2, layers - 1)),
        xgs=dma((layers - 1,)), xgr=dma((layers - 1,)),
        x1s=dma((layers - 1,)), x1r=dma((layers - 1,)),
        x2s=dma((layers - 1,)), x2r=dma((layers - 1,)),
        x3s=dma((layers - 1,)), x3r=dma((layers - 1,)),
        g1s=dma((inner - 1,)), g1r=dma((inner - 1,)),
        g2s=dma((YS - 1,)), g2r=dma((YS - 1,)),
        g3s=dma((YS - 1,)), g3r=dma((YS - 1,)),
        g4s=dma((inner - 1,)), g4r=dma((inner - 1,)),
        swap_send=dma((2, full_d // TILE)), swap_recv=dma((2, full_d // TILE)),
        ls=dma((HALF, Y_CHUNKS)), lr=dma((HALF, Y_CHUNKS)),
        rs=dma((HALF - 1, Y_CHUNKS)), rr=dma((HALF - 1, Y_CHUNKS)),
        yas=dma((YS - 1,)), yar=dma((YS - 1,)),
        ybs=dma((6,)), ybr=dma((6,)),
        zbs=dma((ZS - 1,)), zbr=dma((ZS - 1,)),
        ns=dma((inner - 1,)), nr=dma((inner - 1,)),
        fs=dma((outer - 1,)), fr=dma((outer - 1,)),
    )
    scratch.update(enumerate(gather_sems(2 * layers - 2) + gather_sems(2)))
    names = list(inputs) + list(outputs) + list(scratch)
    cfg = (layers, tokens * lax.axis_size("replica"), base_count)
    fresh, hess = pl.pallas_call(
        functools.partial(main_kernel, cfg, names),
        out_shape=tuple(outputs.values()),
        in_specs=[vmem, hbm, hbm, vmem, vmem],
        out_specs=(vmem, vmem),
        scratch_shapes=list(scratch.values()),
        compiler_params=pltpu.CompilerParams(
            collective_id=1, has_side_effects=True, vmem_limit_bytes=VMEM_BYTES),
    )(*inputs.values())
    return fresh[:, None], hess[:, 0, :base_count + ITERS + 1]


def solution(mesh):
    return jax.shard_map(
        per_device,
        mesh=mesh,
        in_specs=(
            P(None, "replica", None),
            P("section", None, None),
            P("section", None, None),
            P("section", None),
            P(None, "section", None, "replica", None),
        ),
        out_specs=(P(None, "section", None, "replica", None), P()),
        check_vma=False,
    )
```

```python
import functools

import jax
import jax.numpy as jnp
from jax import lax
from jax.experimental import pallas as pl
from jax.experimental.pallas import tpu as pltpu
from jax.sharding import PartitionSpec as P

ITERS = 2
NORM_EPS = 1e-05
VEC_EPS = 1e-06

YS, ZS, CS = 4, 8, 2
HALF = ZS // 2
TILE = 512
MESH = pl.DeviceIdType.MESH
F32 = jnp.float32
BF16 = jnp.bfloat16
VMEM_BYTES = 56 * 1024 * 1024
Y_CHUNKS = 2
ROWS_A = 64


def dot(left, right):
    return jnp.dot(left, right, preferred_element_type=F32)


def dot_t(left, right):
    return lax.dot_general(left, right, (((1,), (1,)), ((), ())), preferred_element_type=F32)


def over_tokens(left, right):
    return lax.dot_general(left, right, (((0,), (0,)), ((), ())), preferred_element_type=F32)


def two_parts(wide):
    high = wide.astype(BF16)
    return high, (wide - high.astype(F32)).astype(BF16)


class Refs:
    def __init__(self, names, refs):
        self.__dict__.update(zip(names, refs, strict=True))


class Place:
    def __init__(self, layers):
        self.layers = layers
        self.sec, rep = lax.axis_index("section"), lax.axis_index("replica")
        self.core = lax.rem(rep, CS)
        self.zed = lax.rem(rep // CS, ZS)
        self.why = rep // (CS * ZS)
        self.inner, self.outer = ZS * CS, layers * YS
        self.here, self.there = self.zed * CS + self.core, self.sec * YS + self.why
        self.sibling = self.device(self.sec, self.why, self.zed, 1 - self.core)

    def device(self, sec, why, zed, core):
        return (sec, (why * ZS + zed) * CS + core)

    def y_at(self, step):
        return lax.rem(self.why + step + YS, YS)

    def z_at(self, step):
        return lax.rem(self.zed + step + ZS, ZS)

    def x(self, step):
        return self.device(lax.rem(self.sec + step, self.layers), self.why, self.zed, self.core)

    def y(self, step):
        return self.device(self.sec, self.y_at(step), self.zed, self.core)

    def z(self, step):
        return self.device(self.sec, self.why, self.z_at(step), self.core)

    def near(self, step):
        return (self.sec, self.why * self.inner + lax.rem(self.here + step, self.inner))

    def far(self, step):
        other = lax.rem(self.there + step, self.outer)
        return (other // YS, lax.rem(other, YS) * self.inner + self.here)

    def slot(self, layer):
        return lax.rem(layer - self.sec + self.layers, self.layers)


def greet(partners):
    barrier = pltpu.get_barrier_semaphore()
    for partner in partners:
        pl.semaphore_signal(barrier, inc=1, device_id=partner, device_id_type=MESH)
    pl.semaphore_wait(barrier, len(partners))


def remote(src, dst, send_sem, recv_sem, partner):
    return pltpu.make_async_remote_copy(
        src_ref=src,
        dst_ref=dst,
        send_sem=send_sem,
        recv_sem=recv_sem,
        device_id=partner,
        device_id_type=MESH,
    )


def exchange(sends, count, partner, source, landing, send, recv):
    copies = []
    for step in range(1, count):
        copy = remote(source(step), landing(step), send.at[step - 1], recv.at[step - 1], partner(step))
        copy.start()
        copies.append(copy)
    sends += copies
    return copies


def arrived(ref, send, recv, at, partner):
    remote(ref, ref, send.at[at], recv.at[at], partner).wait_recv()


def drain(sends):
    for copy in sends:
        copy.wait_send()
    sends.clear()


def merged(*threads):
    threads = list(threads)
    while threads:
        for thread in list(threads):
            try:
                next(thread)
            except StopIteration:
                threads.remove(thread)
                continue
            yield


def finish(thread):
    for _ in thread:
        pass


GATHER_KINDS = 12


def gather_sems(blocks):
    first = blocks // 2
    dma = pltpu.SemaphoreType.DMA
    ring, hand = (ZS - 1, first), (ZS, first)
    return [dma((YS - 1,)), dma((YS - 1,)), dma(ring), dma(ring), dma(hand), dma(hand),
            dma((ZS - 1,)), dma((ZS - 1,)), dma((YS,)), dma((YS,)), dma((YS,)), dma((YS,))]


def ring_steps():
    return [(step, way) for step in range(1, HALF + 1) for way in (1, -1) if way > 0 or step < HALF]


def gather_first(out, blocks, at, sems, sends):
    ysend, yrecv, zsend, zrecv, csend, crecv = sems
    mine = out.at[pl.ds(blocks[0], len(blocks)), at.why, at.zed, at.core]
    exchange(sends, YS, at.y, lambda step: mine, lambda step: mine, ysend, yrecv)

    def bundle(chunk, z, core):
        return out.at[blocks[chunk], :, z, core]

    steps = ring_steps()

    def index(step, way):
        return steps.index((step, way))

    def hand_index(step, way):
        return 0 if step == 0 else index(step, way) + 1

    def send(step, way, chunk):
        view = bundle(chunk, at.z_at(-way * (step - 1)), at.core)
        copy = remote(view, view, zsend.at[index(step, way), chunk], zrecv.at[index(step, way), chunk],
                      at.z(way))
        copy.start()
        sends.append(copy)

    def hand_on(step, way, chunk):
        view = bundle(chunk, at.z_at(-way * step), at.core)
        copy = remote(view, view, csend.at[hand_index(step, way), chunk],
                      crecv.at[hand_index(step, way), chunk], at.sibling)
        copy.start()
        sends.append(copy)

    yield
    for step in range(1, YS):
        block = out.at[pl.ds(blocks[0], len(blocks)), at.y_at(-step), at.zed, at.core]
        arrived(block, ysend, yrecv, step - 1, at.sibling)
    for chunk in range(len(blocks)):
        send(1, 1, chunk)
        send(1, -1, chunk)
    for chunk in range(len(blocks)):
        hand_on(0, 1, chunk)
    for step in range(1, HALF + 1):
        for chunk in range(len(blocks)):
            yield
            for way in (1, -1):
                if (step, way) not in steps:
                    continue
                view = bundle(chunk, at.z_at(-way * step), at.core)
                remote(view, view, zsend.at[index(step, way), chunk], zrecv.at[index(step, way), chunk],
                       at.sibling).wait_recv()
                if (step + 1, way) in steps:
                    send(step + 1, way, chunk)
                hand_on(step, way, chunk)
    for step, way in [(0, 1)] + steps:
        yield
        for chunk in range(len(blocks)):
            view = bundle(chunk, at.z_at(-way * step), 1 - at.core)
            remote(view, view, csend.at[hand_index(step, way), chunk],
                   crecv.at[hand_index(step, way), chunk], at.sibling).wait_recv()


def gather_second(out, blocks, at, sems, sends, pauses):
    zsend, zrecv, ysend, yrecv, csend, crecv = sems
    span = pl.ds(blocks[0], len(blocks))

    def view(z):
        return out.at[span, at.why, z, at.core]

    def bundle(step, core, part=None):
        zeds = pl.ds(0, ZS) if part is None else pl.ds(part * HALF, HALF)
        return out.at[span, at.y_at(step), zeds, core]

    def along(ref, idx, way):
        copy = remote(ref, ref, ysend.at[idx], yrecv.at[idx], at.y(way))
        copy.start()
        sends.append(copy)

    def hand_on(step, idx):
        ref = bundle(step, at.core)
        copy = remote(ref, ref, csend.at[idx], crecv.at[idx], at.sibling)
        copy.start()
        sends.append(copy)

    exchange(sends, ZS, at.z, lambda step: view(at.zed), lambda step: view(at.zed), zsend, zrecv)
    for _ in range(pauses[0]):
        yield
    for step in range(1, ZS):
        arrived(view(at.z_at(-step)), zsend, zrecv, step - 1, at.sibling)
    along(bundle(0, at.core), 0, 1)
    along(bundle(0, at.core), 1, -1)
    hand_on(0, 0)
    for _ in range(pauses[1]):
        yield
    arrived(bundle(-1, at.core), ysend, yrecv, 0, at.sibling)
    along(bundle(-1, at.core, 0), 2, 1)
    arrived(bundle(1, at.core), ysend, yrecv, 1, at.sibling)
    along(bundle(1, at.core, 1), 3, -1)
    hand_on(-1, 1)
    hand_on(1, 2)
    for _ in range(pauses[2]):
        yield
    arrived(bundle(2, at.core, 0), ysend, yrecv, 2, at.sibling)
    arrived(bundle(2, at.core, 1), ysend, yrecv, 3, at.sibling)
    hand_on(2, 3)
    for idx, step in enumerate((0, -1, 1, 2)):
        yield
        arrived(bundle(step, 1 - at.core), csend, crecv, idx, at.sibling)


def gather(out, start, count, at, sems, sends):
    half = count // 2
    first = list(range(start, start + half))
    second = list(range(start + half, start + count))
    chunks = len(first)
    pauses = (chunks + 2, 2 * chunks - 1, chunks)
    return merged(gather_second(out, second, at, sems[6:], sends, pauses),
                  gather_first(out, first, at, sems[:6], sends))


def row_block(ref, block, idx):
    per = TILE // (CS * 64)
    wide = ref[block, idx // (ZS // per), pl.ds((idx % (ZS // per)) * per, per)]
    return wide.reshape(TILE, 128)


def tiles(full_d, body, between=None, parts=1):
    def step(idx, carry):
        body(idx, pl.ds(pl.multiple_of(idx * TILE, TILE), TILE))
        return carry
    count = full_d // TILE // parts
    for part in range(parts):
        lax.fori_loop(part * count, (part + 1) * count, step, 0)
        if between is not None:
            between()


def every_up(ref, at, idx):
    return jnp.concatenate(
        [row_block(ref.weights, 2 * at.slot(layer) + 1, idx) for layer in range(at.layers)], axis=1)


def lane_sums(wide):
    return sum(wide[:, start:start + 128] for start in range(0, TILE, 128))


def primal(ref, at, full_d, between):
    layers, sec = at.layers, at.sec
    tokens = ref.rows.shape[0]
    acc, along = ref.acc, ref.along
    along[0] = jnp.zeros((tokens, 128), F32)

    def rows_of(layer, cols):
        return ref.rows[:, cols] if layer == 0 else ref.every_row[layer - 1, :, cols]

    def square(idx, cols):
        wide = ref.rows[:, cols].astype(F32)
        along[0] += lane_sums(wide * wide)
    tiles(full_d, square, between)
    for layer in range(layers):
        down, up = 2 * at.slot(layer), 2 * at.slot(layer) + 1
        mean = jnp.sum(along[0], axis=-1, keepdims=True) * (1.0 / full_d)
        inv = lax.rsqrt(mean + NORM_EPS)
        acc[0] = jnp.zeros((tokens, 128), F32)

        def project(idx, cols):
            gain = ref.gains[at.slot(layer), :, cols]
            piece = (rows_of(layer, cols).astype(F32) * inv * gain).astype(BF16)

            @pl.when(sec == layer)
            def _():
                ref.normed[:, cols] = piece
            acc[0] += dot(piece, row_block(ref.weights, down, idx))
        tiles(full_d, project, between, 2)
        pre = acc[0]
        sig = jax.nn.sigmoid(pre)
        act = (pre * sig).astype(BF16)
        ref.hidden[:, layer * 128:(layer + 1) * 128] = act

        @pl.when(sec == layer)
        def _():
            ref.own_hidden[...] = act
        ref.pre_act[layer] = pre
        ref.slope[layer] = sig + pre * sig * (1.0 - sig)
        ref.inv_rms[layer] = jnp.broadcast_to(inv, (tokens, 128))
        along[0] = jnp.zeros((tokens, 128), F32)
        if layer + 1 < layers:
            def forward(idx, cols):
                wide = rows_of(layer, cols).astype(F32)
                wide = wide + dot_t(act, row_block(ref.weights, up, idx))
                rounded = wide.astype(BF16)
                ref.every_row[layer, :, cols] = rounded
                again = rounded.astype(F32)
                along[0] += lane_sums(again * again)
            tiles(full_d, forward, between, 2)
    ref.gram[...] = over_tokens(ref.hidden[...], ref.own_hidden[...])
    between()


def weight_products(ref, at, full_d, between):
    layers, sec = at.layers, at.sec
    part = ref.rows.shape[0] // layers
    mine = pl.ds(pl.multiple_of(sec * part, part), part)
    ref.uu[...] = jnp.zeros_like(ref.uu)
    ref.ud[...] = jnp.zeros_like(ref.ud)
    ref.row_up[...] = jnp.zeros_like(ref.row_up)

    def grams(idx, cols):
        every = every_up(ref, at, idx)
        turned = every.T
        ref.uu[...] += dot(turned, every)
        pair_at = 0
        for layer in range(1, layers):
            width = layer * 128
            gain = ref.gains[at.slot(layer), :, cols]
            high, low = two_parts(turned[:width].astype(F32) * gain)
            down = row_block(ref.weights, 2 * at.slot(layer), idx)
            pair = dot(high, down) + dot(low, down)
            block = dot(ref.every_row[layer - 1, mine, cols], every[:, :width])
            for k in range(layer):
                ref.ud[pair_at] += pair[k * 128:(k + 1) * 128]
                ref.row_up[pair_at] += block[:, k * 128:(k + 1) * 128]
                pair_at += 1
    tiles(full_d, grams, between, 4)
    ref.uu_high[...], ref.uu_low[...] = two_parts(ref.uu[...])
    ref.ud_high[...], ref.ud_low[...] = two_parts(ref.ud[...])


def recurrence(tan_base, back_base, pre_act, slope, inv_rms, row_up, up_up, up_down, full_d):
    layers = len(tan_base)
    tan_act = []
    for layer in range(layers):
        tan_pre = tan_base[layer]
        if layer > 0:
            moved = sum(dot(tan_act[k], up_down[k][layer][0]) + dot(tan_act[k], up_down[k][layer][1])
                        for k in range(layer))
            along = sum(jnp.sum(tan_act[k].astype(F32) * row_up[layer][k], axis=-1, keepdims=True)
                        for k in range(layer))
            inv = inv_rms[layer]
            tan_pre = tan_pre + inv * moved - (inv * inv * (1.0 / full_d)) * along * pre_act[layer]
        tan_act.append((tan_pre * slope[layer]).astype(BF16))
    every = jnp.concatenate(tan_act, axis=1)
    back_all = dot(every, up_up[0]) + dot(every, up_up[1])
    back_pre, moved_back, pull = {}, {}, {}
    for layer in reversed(range(layers)):
        back_act = back_base[layer] + back_all[:, layer * 128:(layer + 1) * 128]
        for k in range(layer + 1, layers):
            back_act = back_act + dot_t(moved_back[k], up_down[layer][k][0])
            back_act = back_act + dot_t(moved_back[k], up_down[layer][k][1])
            back_act = back_act - pull[k] * row_up[k][layer]
        piece = (back_act * slope[layer]).astype(BF16)
        wide = piece.astype(F32)
        inv = inv_rms[layer]
        back_pre[layer] = piece
        moved_back[layer] = (wide * inv).astype(BF16)
        pull[layer] = inv * inv * (1.0 / full_d) * jnp.sum(wide * pre_act[layer], axis=-1, keepdims=True)
    return tan_act + [back_pre[layer] for layer in range(layers)]


def token_terms(ref, at, full_d):
    layers, sec = at.layers, at.sec
    acc, along = ref.acc, ref.along
    acc[...] = jnp.zeros_like(acc)
    ref.acc_up[...] = jnp.zeros_like(ref.acc_up)
    along[...] = jnp.zeros_like(along)
    own_hidden = ref.own_hidden[...]
    part = own_hidden.shape[0] // layers

    def body(idx, cols):
        acc[0] += dot(ref.normed[:, cols], row_block(ref.vector, 0, idx))
        spread = dot_t(own_hidden, row_block(ref.vector, 1, idx))
        rounded = spread.astype(BF16)
        ref.acc_up[...] += dot(rounded, every_up(ref, at, idx))
        for layer in range(1, layers):
            scaled = (spread * ref.gains[at.slot(layer), :, cols]).astype(BF16)
            acc[layer] += dot(scaled, row_block(ref.weights, 2 * at.slot(layer), idx))
            along[layer] += lane_sums(ref.every_row[layer - 1, :, cols].astype(F32) * spread)
    tiles(full_d, body)
    base = acc[0]

    def put(block, value):
        value = value.astype(BF16)
        for quarter in range(layers):
            ref.pay[quarter, :, block * 128:(block + 1) * 128] = value[quarter * part:(quarter + 1) * part]
    for layer in range(layers):
        own = jnp.where(sec == layer, base, 0.0)
        if layer > 0:
            inv = ref.inv_rms[layer]
            reach = jnp.sum(along[layer], axis=-1, keepdims=True)
            later = inv * acc[layer] - (inv * inv * (1.0 / full_d)) * reach * ref.pre_act[layer]
            own = own + jnp.where(sec < layer, later, 0.0)
        put(layer, own)
        put(layers + layer, ref.acc_up[:, layer * 128:(layer + 1) * 128])


def gradient_terms(ref, at, full_d):
    layers, sec = at.layers, at.sec
    res = ref.result
    part = res.shape[1]
    tokens = part * layers

    def column(block):
        return jnp.concatenate([res[q, :, block * 128:(block + 1) * 128] for q in range(layers)], axis=0)
    back = [column(layers + layer) for layer in range(layers)]
    pulls, moved = [], []
    for layer in range(layers):
        inv = ref.inv_rms[layer]
        wide = back[layer].astype(F32)
        pull = inv * inv * (1.0 / full_d) * jnp.sum(wide * ref.pre_act[layer], axis=-1, keepdims=True)
        pulls.append(jnp.where(sec < layer, pull, 0.0))
        moved.append(jnp.where(sec < layer, wide * inv, 0.0).astype(BF16))
    acts = []
    later = jnp.zeros((tokens, 128), F32)
    for layer in reversed(range(layers)):
        old = ref.hidden[:, layer * 128:(layer + 1) * 128].astype(F32)
        acts.insert(0, (column(layer).astype(F32) - later * old).astype(BF16))
        later = later + pulls[layer]
    total = later[:, :1]
    act_cat = jnp.concatenate(acts, axis=1)
    own_back = back[0]
    for layer in range(1, layers):
        own_back = jnp.where(sec == layer, back[layer], own_back)
    own_hidden = ref.own_hidden[...]
    per = TILE // (CS * 64)

    def body(idx, cols):
        cot = dot_t(act_cat, every_up(ref, at, idx)) - total * ref.rows[:, cols].astype(F32)
        for layer in range(1, layers):
            cot = cot + (dot_t(moved[layer], row_block(ref.weights, 2 * at.slot(layer), idx))
                         * ref.gains[at.slot(layer), :, cols])
        where = (idx // (ZS // per), pl.ds((idx % (ZS // per)) * per, per))
        up = over_tokens(cot.astype(BF16), own_hidden).reshape(per, CS, 64, 128)
        down = over_tokens(ref.normed[:, cols], own_back).reshape(per, CS, 64, 128)
        ref.part[where] = jnp.concatenate([down, up], axis=2)
        swap_copy(ref, at, idx).start()
    tiles(full_d, body)


def swap_copy(ref, at, idx):
    per = TILE // (CS * 64)
    where = (idx // (ZS // per), pl.ds((idx % (ZS // per)) * per, per))
    return remote(ref.part.at[where + (1 - at.core,)], ref.swap.at[where], ref.swap_send.at[idx],
                  ref.swap_recv.at[idx], at.sibling)


def scatter_first(ref, at, sends, done):
    left_in, right_in, y_in = ref.left_in, ref.right_in, ref.y_a
    size = YS // Y_CHUNKS

    def chunk_of(chunk):
        return pl.ds(chunk * size, size)

    def chip_sum(z, chunk):
        span = chunk_of(chunk)
        return ref.swap[span, z, :ROWS_A] + ref.part[span, z, at.core, :ROWS_A]

    def left(step, chunk):
        z = at.z_at(step - HALF - 1)
        return remote(ref.out_a.at[chunk_of(chunk), z], left_in.at[step - 1, chunk_of(chunk)],
                      ref.ls.at[step - 1, chunk], ref.lr.at[step - 1, chunk], at.z(-1))

    def right(step, chunk):
        z = at.z_at(HALF - step)
        return remote(ref.out_a.at[chunk_of(chunk), z], right_in.at[step - 1, chunk_of(chunk)],
                      ref.rs.at[step - 1, chunk], ref.rr.at[step - 1, chunk], at.z(1))

    def go(copy):
        copy.start()
        sends.append(copy)

    for step in range(1, HALF + 1):
        for chunk in range(Y_CHUNKS):
            if step > 1:
                yield
            span = chunk_of(chunk)
            z = at.z_at(step - HALF - 1)
            value = chip_sum(z, chunk)
            if step > 1:
                left(step - 1, chunk).wait_recv()
                value = value + left_in[step - 2, span]
            ref.out_a[span, z] = value
            go(left(step, chunk))
            if step < HALF:
                z = at.z_at(HALF - step)
                value = chip_sum(z, chunk)
                if step > 1:
                    right(step - 1, chunk).wait_recv()
                    value = value + right_in[step - 2, span]
                ref.out_a[span, z] = value
                go(right(step, chunk))
    yield
    for chunk in range(Y_CHUNKS):
        span = chunk_of(chunk)
        value = chip_sum(at.zed, chunk)
        right(HALF - 1, chunk).wait_recv()
        value = value + right_in[HALF - 2, span]
        left(HALF, chunk).wait_recv()
        ref.out_a[span, at.zed] = value + left_in[HALF - 1, span]

    copies = exchange(sends, YS, at.y, lambda step: ref.out_a.at[at.y_at(step), at.zed],
                      lambda step: y_in.at[step - 1], ref.yas, ref.yar)
    yield
    value = ref.out_a[at.why, at.zed]
    for step, copy in enumerate(copies):
        copy.wait_recv()
        value = value + y_in[step]
    done.append(value)


def scatter_second(ref, at, sends, done):
    halves = (pl.ds(0, HALF), pl.ds(HALF, HALF))
    out = ref.out_b

    def chip_sum(step, half):
        y = at.y_at(step)
        return ref.swap[y, halves[half], ROWS_A:] + ref.part[y, halves[half], at.core, ROWS_A:]

    def go(src, dst, idx, way):
        copy = remote(src, dst, ref.ybs.at[idx], ref.ybr.at[idx], at.y(way))
        copy.start()
        sends.append(copy)

    def took(dst, idx):
        arrived(dst, ref.ybs, ref.ybr, idx, at.sibling)

    def view(step, half):
        return out.at[at.y_at(step), halves[half]]

    out[at.y_at(2), halves[0]] = chip_sum(2, 0)
    go(view(2, 0), ref.chain.at[0], 0, 1)
    out[at.y_at(2), halves[1]] = chip_sum(2, 1)
    go(view(2, 1), ref.chain.at[1], 1, -1)
    out[at.y_at(1), halves[1]] = chip_sum(1, 1)
    go(view(1, 1), ref.from_low.at[halves[1]], 2, 1)
    out[at.y_at(-1), halves[0]] = chip_sum(-1, 0)
    go(view(-1, 0), ref.from_high.at[halves[0]], 3, -1)
    yield
    yield
    took(ref.chain.at[0], 0)
    out[at.y_at(1), halves[0]] = chip_sum(1, 0) + ref.chain[0]
    go(view(1, 0), ref.from_low.at[halves[0]], 4, 1)
    took(ref.chain.at[1], 1)
    out[at.y_at(-1), halves[1]] = chip_sum(-1, 1) + ref.chain[1]
    go(view(-1, 1), ref.from_high.at[halves[1]], 5, -1)
    yield
    yield
    yield
    took(ref.from_low.at[halves[1]], 2)
    took(ref.from_high.at[halves[0]], 3)
    took(ref.from_low.at[halves[0]], 4)
    took(ref.from_high.at[halves[1]], 5)
    for half in range(2):
        out[at.why, halves[half]] = (
            chip_sum(0, half) + ref.from_low[halves[half]] + ref.from_high[halves[half]])
    copies = exchange(sends, ZS, at.z, lambda step: out.at[at.why, at.z_at(step)],
                      lambda step: ref.z_b.at[step - 1], ref.zbs, ref.zbr)
    yield
    yield
    yield
    value = out[at.why, at.zed]
    for step, copy in enumerate(copies):
        copy.wait_recv()
        value = value + ref.z_b[step]
    done.append(value)


def scatter_sum(ref, at, full_d, sends):
    for idx in range(full_d // TILE):
        copy = swap_copy(ref, at, idx)
        copy.wait_recv()
        sends.append(copy)
    done_a, done_b = [], []
    finish(merged(scatter_second(ref, at, sends, done_b), scatter_first(ref, at, sends, done_a)))
    both = jnp.concatenate([done_a[0], done_b[0]], axis=0)
    return both[:64], both[64:]


def gram_steps(ref, at, sends):
    gram, whole = ref.gram, ref.hidden_gram
    piece = gram.shape[0] // at.inner
    small = piece // YS

    def rows(index, size):
        return pl.ds(pl.multiple_of(index * size, size), size)

    copies = exchange(sends, at.inner, at.near,
                      lambda step: gram.at[rows(lax.rem(at.here + step, at.inner), piece)],
                      lambda step: ref.gram_in.at[step - 1], ref.g1s, ref.g1r)
    yield
    value = gram[rows(at.here, piece), :]
    for step, copy in enumerate(copies):
        copy.wait_recv()
        value = value + ref.gram_in[step]
    ref.gram_sum[...] = value
    copies = exchange(sends, YS, at.y, lambda step: ref.gram_sum.at[rows(at.y_at(step), small)],
                      lambda step: ref.gram_in2.at[step - 1], ref.g2s, ref.g2r)
    yield
    own = rows(at.why, small)
    value = ref.gram_sum[own, :]
    for step, copy in enumerate(copies):
        copy.wait_recv()
        value = value + ref.gram_in2[step]
    ref.gram_out[own, :] = value
    exchange(sends, YS, at.y, lambda step: ref.gram_out.at[own], lambda step: ref.gram_out.at[own],
             ref.g3s, ref.g3r)
    yield
    for step in range(1, YS):
        arrived(ref.gram_out.at[rows(at.y_at(-step), small)], ref.g3s, ref.g3r, step - 1, at.sibling)
    mine = rows(at.here, piece)
    whole[mine, :] = ref.gram_out[...]
    exchange(sends, at.inner, at.near, lambda step: ref.gram_out, lambda step: whole.at[mine],
             ref.g4s, ref.g4r)
    yield
    for step in range(1, at.inner):
        source = rows(lax.rem(at.here + at.inner - step, at.inner), piece)
        arrived(whole.at[source], ref.g4s, ref.g4r, step - 1, at.sibling)


def sum_all(ref, at, line, sends):
    vec, near, far, half_sum = ref.vec, ref.near, ref.far, ref.half_sum
    vec[...] = jnp.broadcast_to(line, vec.shape)
    exchange(sends, at.inner, at.near, lambda step: vec, lambda step: near.at[at.here], ref.ns, ref.nr)
    near[at.here] = vec[...]
    for step in range(1, at.inner):
        slot = near.at[lax.rem(at.here + at.inner - step, at.inner)]
        arrived(slot, ref.ns, ref.nr, step - 1, at.sibling)
    half_sum[...] = jnp.sum(near[...], axis=0)
    exchange(sends, at.outer, at.far, lambda step: half_sum, lambda step: far.at[at.there], ref.fs, ref.fr)
    far[at.there] = half_sum[...]
    for step in range(1, at.outer):
        slot = far.at[lax.rem(at.there + at.outer - step, at.outer)]
        arrived(slot, ref.fs, ref.fr, step - 1, at.sibling)
    return jnp.sum(far[...], axis=0)[:1]


def put_vector(ref, at, down_rows, up_rows, full_d, rank, sends):
    ref.shard[0] = (down_rows * (full_d ** -0.5)).astype(BF16)
    ref.shard[1] = (up_rows * (rank ** -0.5)).astype(BF16)
    ref.vector[:, at.why, at.zed, at.core] = ref.shard[...]
    ref.ups[0] = ref.shard[1]
    exchange(sends, at.layers, at.x, lambda step: ref.shard.at[1],
             lambda step: ref.ups.at[at.layers - step], ref.x3s, ref.x3r)


def ups_arrived(ref, at):
    for step in range(1, at.layers):
        arrived(ref.ups.at[at.layers - step], ref.x3s, ref.x3r, step - 1, at.sibling)


def curvature(ref, at, full_d, sends, between):
    layers, sec = at.layers, at.sec
    token_terms(ref, at, full_d)
    pay = ref.pay
    copies = exchange(sends, layers, at.x, lambda step: pay.at[lax.rem(sec + step, layers)],
                      lambda step: ref.pay_in.at[step - 1], ref.x1s, ref.x1r)
    total = pay[sec].astype(F32)
    for step, copy in enumerate(copies):
        copy.wait_recv()
        total = total + ref.pay_in[step].astype(F32)
    between()
    row_up = {}
    up_down = {k: {} for k in range(layers)}
    idx = 0
    for layer in range(layers):
        for k in range(layer):
            row_up.setdefault(layer, {})[k] = ref.row_up[idx]
            up_down[k][layer] = (ref.ud_high[idx], ref.ud_low[idx])
            idx += 1
    part = pay.shape[1]
    mine = pl.ds(pl.multiple_of(sec * part, part), part)
    pieces = recurrence(
        [total[:, start * 128:(start + 1) * 128] for start in range(layers)],
        [total[:, start * 128:(start + 1) * 128] for start in range(layers, 2 * layers)],
        [ref.pre_act[layer, mine, :] for layer in range(layers)],
        [ref.slope[layer, mine, :] for layer in range(layers)],
        [ref.inv_rms[layer, mine, :] for layer in range(layers)],
        row_up, (ref.uu_high[...], ref.uu_low[...]), up_down, full_d)
    result = ref.result
    result[sec] = jnp.concatenate(pieces, axis=1)
    own = result.at[sec]
    exchange(sends, layers, at.x, lambda step: own, lambda step: own, ref.x2s, ref.x2r)
    between()
    for step in range(1, layers):
        arrived(result.at[lax.rem(sec + layers - step, layers)], ref.x2s, ref.x2r, step - 1, at.sibling)
    between()
    gradient_terms(ref, at, full_d)
    return scatter_sum(ref, at, full_d, sends)


def main_kernel(cfg, names, *refs):
    layers, tokens_all, base_count = cfg
    ref = Refs(names, refs)
    at = Place(layers)
    full_d, rank = ref.rows.shape[1], ref.down.shape[-1]
    sends = []
    lane = lax.broadcasted_iota(jnp.int32, (1, 128), 1)
    copies = [pltpu.make_async_copy(ref.down, ref.weights.at[0], ref.local.at[0]),
              pltpu.make_async_copy(ref.up, ref.weights.at[1], ref.local.at[1])]
    for copy in copies:
        copy.start()
    ref.gains[0] = ref.gain[...]
    greet([at.near(step) for step in range(1, at.inner)] + [at.far(step) for step in range(1, at.outer)])

    for block, source in enumerate((ref.down, ref.up)):
        row = source.at[at.why, at.zed, at.core]
        exchange(sends, layers, at.x, lambda step: row,
                 lambda step: ref.weights.at[2 * (layers - step) + block, at.why, at.zed, at.core],
                 ref.xws.at[block], ref.xwr.at[block])
    exchange(sends, layers, at.x, lambda step: ref.gain, lambda step: ref.gains.at[layers - step],
             ref.xgs, ref.xgr)
    put_vector(ref, at, ref.basis[base_count - 1, 0], ref.basis[base_count - 1, 1], full_d, rank, sends)
    for step in range(1, layers):
        for block in range(2):
            arrived(ref.weights.at[2 * (layers - step) + block, at.why, at.zed, at.core],
                    ref.xws.at[block], ref.xwr.at[block], step - 1, at.sibling)
    sems = [ref.__dict__[key] for key in range(2 * GATHER_KINDS)]
    finish(gather(ref.weights, 2, 2 * layers - 2, at, sems[:GATHER_KINDS], sends))
    for step in range(1, layers):
        arrived(ref.gains.at[layers - step], ref.xgs, ref.xgr, step - 1, at.sibling)
    for copy in copies:
        copy.wait()
    moving = gather(ref.vector, 0, 2, at, sems[GATHER_KINDS:], sends)

    calls = []

    def move():
        calls.append(None)
        if len(calls) % 2 == 0:
            next(moving, None)
    next(moving, None)
    next(moving, None)
    primal(ref, at, full_d, move)
    weight_products(ref, at, full_d, move)
    finish(moving)
    ups_arrived(ref, at)
    drain(sends)

    norm = 1.0 / tokens_all
    scales = (full_d ** -0.5, rank ** -0.5)
    held = [(ref.basis[k, 0], ref.basis[k, 1]) for k in range(base_count)]
    gram_slots = {}

    def gram_at(k, j):
        return gram_slots[max(k, j), min(k, j)]

    def inner_sum(left, right):
        both = left[0] * right[0] + left[1] * right[1]
        return jnp.sum(jnp.sum(both, axis=0, keepdims=True), axis=1, keepdims=True)

    for it in range(ITERS):
        count = base_count + it
        summing = gram_steps(ref, at, sends) if it == 0 else iter(())
        next(summing, None)
        sum_a, sum_b = curvature(ref, at, full_d, sends, lambda: next(summing, None))
        finish(summing)
        for layer in range(layers):
            wide = ref.hidden_gram[layer * rank:(layer + 1) * rank, :]
            high = wide.astype(BF16)
            rest = wide - high.astype(F32)
            middle, low = two_parts(rest)
            ups = ref.ups[at.slot(layer)]
            sum_b = sum_b + dot(ups, high) + dot(ups, middle) + dot(ups, low)
        image = [sum_a * (scales[0] * norm), sum_b * (scales[1] * norm)]

        pairs = [(k, j) for k in range(count) for j in range(k + 1) if (k, j) not in gram_slots]
        values = [inner_sum(item, image) for item in held] + [inner_sum(image, image)]
        values += [inner_sum(held[k], held[j]) for k, j in pairs]
        line = jnp.zeros((1, 128), F32)
        for place, value in enumerate(values):
            line = jnp.where(lane == place, value, line)
        line = sum_all(ref, at, line, sends) * (1.0 / (layers * 2 * full_d * rank))
        totals = [jnp.sum(jnp.where(lane == place, line, 0.0), axis=1, keepdims=True)
                  for place in range(len(values))]
        first_coef, image_square = totals[:count], totals[count]
        gram_slots.update(zip(pairs, totals[count + 1:]))
        coef, length_square = [], image_square
        for k in range(count):
            again = sum(gram_at(k, j) * first_coef[j] for j in range(count))
            coef.append(first_coef[k] + (first_coef[k] - again))
        for k in range(count):
            mixed = sum(gram_at(k, j) * coef[j] for j in range(count))
            length_square = length_square + coef[k] * (mixed - 2.0 * first_coef[k])
        length = jnp.sqrt(jnp.maximum(length_square, 0.0) + VEC_EPS)
        fresh = []
        for block in range(2):
            clean = image[block]
            for k in range(count):
                clean = clean - coef[k] * held[k][block]
            fresh.append(clean / length)
            ref.fresh[it, block] = fresh[block]
        line = jnp.zeros((1, 128), F32)
        for k in range(count):
            line = jnp.where(lane == k, coef[k], line)
        line = jnp.where(lane == base_count + ITERS, length, line)
        ref.hess[it:it + 1, :] = line[:, :base_count + ITERS + 1]
        drain(sends)
        if it + 1 < ITERS:
            held.append((ref.fresh[it, 0], ref.fresh[it, 1]))
            put_vector(ref, at, fresh[0], fresh[1], full_d, rank, sends)
            finish(gather(ref.vector, 0, 2, at, sems[GATHER_KINDS:], sends))
            ups_arrived(ref, at)
            drain(sends)


def per_device(hidden_in, down_weight, up_weight, norm_gain, krylov_basis):
    layers = lax.axis_size("section")
    micro, tok, full_d = hidden_in.shape
    rank = down_weight.shape[2]
    tokens = micro * tok
    part = tokens // layers
    basis = krylov_basis[:, 0]
    base_count, _, rows, _ = basis.shape
    split = (YS, ZS, CS, rows, rank)
    vmem = pl.BlockSpec(memory_space=pltpu.VMEM)
    hbm = pl.BlockSpec(memory_space=pl.ANY)
    dma = pltpu.SemaphoreType.DMA
    inner, outer = ZS * CS, layers * YS
    pairs = layers * (layers - 1) // 2
    wide = layers * rank
    piece = wide // inner
    rows_b = 2 * rows - ROWS_A

    inputs = dict(
        rows=hidden_in.reshape(tokens, full_d),
        down=down_weight[0].reshape(split),
        up=up_weight[0].reshape(split),
        gain=norm_gain,
        basis=basis,
    )
    outputs = dict(
        fresh=jax.ShapeDtypeStruct((ITERS, 2, rows, rank), F32),
        hess=jax.ShapeDtypeStruct((ITERS, base_count + ITERS + 1), F32),
    )
    scratch = dict(
        weights=pltpu.VMEM((2 * layers,) + split, BF16),
        vector=pltpu.VMEM((2,) + split, BF16),
        gains=pltpu.VMEM((layers, 1, full_d), F32),
        ups=pltpu.VMEM((layers, rows, rank), BF16),
        shard=pltpu.VMEM((2, rows, rank), BF16),
        every_row=pltpu.VMEM((layers - 1, tokens, full_d), BF16),
        normed=pltpu.VMEM((tokens, full_d), BF16),
        hidden=pltpu.VMEM((tokens, wide), BF16),
        own_hidden=pltpu.VMEM((tokens, rank), BF16),
        pre_act=pltpu.VMEM((layers, tokens, rank), F32),
        slope=pltpu.VMEM((layers, tokens, rank), F32),
        inv_rms=pltpu.VMEM((layers, tokens, 128), F32),
        row_up=pltpu.VMEM((pairs, part, rank), F32),
        uu=pltpu.VMEM((wide, wide), F32),
        ud=pltpu.VMEM((pairs, rank, rank), F32),
        uu_high=pltpu.VMEM((wide, wide), BF16),
        uu_low=pltpu.VMEM((wide, wide), BF16),
        ud_high=pltpu.VMEM((pairs, rank, rank), BF16),
        ud_low=pltpu.VMEM((pairs, rank, rank), BF16),
        gram=pltpu.VMEM((wide, rank), F32),
        hidden_gram=pltpu.VMEM((wide, rank), F32),
        gram_in=pltpu.VMEM((inner - 1, piece, rank), F32),
        gram_sum=pltpu.VMEM((piece, rank), F32),
        gram_in2=pltpu.VMEM((YS - 1, piece // YS, rank), F32),
        gram_out=pltpu.VMEM((piece, rank), F32),
        acc=pltpu.VMEM((layers, tokens, rank), F32),
        acc_up=pltpu.VMEM((tokens, wide), F32),
        along=pltpu.VMEM((layers, tokens, 128), F32),
        pay=pltpu.VMEM((layers, part, 2 * wide), BF16),
        pay_in=pltpu.VMEM((layers - 1, part, 2 * wide), BF16),
        result=pltpu.VMEM((layers, part, 2 * wide), BF16),
        part=pltpu.VMEM((YS, ZS, CS, 2 * rows, rank), F32),
        swap=pltpu.VMEM((YS, ZS, 2 * rows, rank), F32),
        out_a=pltpu.VMEM((YS, ZS, ROWS_A, rank), F32),
        out_b=pltpu.VMEM((YS, ZS, rows_b, rank), F32),
        left_in=pltpu.VMEM((HALF, YS, ROWS_A, rank), F32),
        right_in=pltpu.VMEM((HALF - 1, YS, ROWS_A, rank), F32),
        y_a=pltpu.VMEM((YS - 1, ROWS_A, rank), F32),
        chain=pltpu.VMEM((2, HALF, rows_b, rank), F32),
        from_low=pltpu.VMEM((ZS, rows_b, rank), F32),
        from_high=pltpu.VMEM((ZS, rows_b, rank), F32),
        z_b=pltpu.VMEM((ZS - 1, rows_b, rank), F32),
        vec=pltpu.VMEM((8, 128), F32),
        near=pltpu.VMEM((inner, 8, 128), F32),
        far=pltpu.VMEM((outer, 8, 128), F32),
        half_sum=pltpu.VMEM((8, 128), F32),
        local=dma((2,)),
        xws=dma((2, layers - 1)), xwr=dma((2, layers - 1)),
        xgs=dma((layers - 1,)), xgr=dma((layers - 1,)),
        x1s=dma((layers - 1,)), x1r=dma((layers - 1,)),
        x2s=dma((layers - 1,)), x2r=dma((layers - 1,)),
        x3s=dma((layers - 1,)), x3r=dma((layers - 1,)),
        g1s=dma((inner - 1,)), g1r=dma((inner - 1,)),
        g2s=dma((YS - 1,)), g2r=dma((YS - 1,)),
        g3s=dma((YS - 1,)), g3r=dma((YS - 1,)),
        g4s=dma((inner - 1,)), g4r=dma((inner - 1,)),
        swap_send=dma((full_d // TILE,)), swap_recv=dma((full_d // TILE,)),
        ls=dma((HALF, Y_CHUNKS)), lr=dma((HALF, Y_CHUNKS)),
        rs=dma((HALF - 1, Y_CHUNKS)), rr=dma((HALF - 1, Y_CHUNKS)),
        yas=dma((YS - 1,)), yar=dma((YS - 1,)),
        ybs=dma((6,)), ybr=dma((6,)),
        zbs=dma((ZS - 1,)), zbr=dma((ZS - 1,)),
        ns=dma((inner - 1,)), nr=dma((inner - 1,)),
        fs=dma((outer - 1,)), fr=dma((outer - 1,)),
    )
    scratch.update(enumerate(gather_sems(2 * layers - 2) + gather_sems(2)))
    names = list(inputs) + list(outputs) + list(scratch)
    cfg = (layers, tokens * lax.axis_size("replica"), base_count)
    fresh, hess = pl.pallas_call(
        functools.partial(main_kernel, cfg, names),
        out_shape=tuple(outputs.values()),
        in_specs=[vmem, hbm, hbm, vmem, vmem],
        out_specs=(vmem, vmem),
        scratch_shapes=list(scratch.values()),
        compiler_params=pltpu.CompilerParams(
            collective_id=1, has_side_effects=True, vmem_limit_bytes=VMEM_BYTES),
    )(*inputs.values())
    return fresh[:, None], hess


def solution(mesh):
    return jax.shard_map(
        per_device,
        mesh=mesh,
        in_specs=(
            P(None, "replica", None),
            P("section", None, None),
            P("section", None, None),
            P("section", None),
            P(None, "section", None, "replica", None),
        ),
        out_specs=(P(None, "section", None, "replica", None), P()),
        check_vma=False,
    )
```

```python
import functools

import jax
import jax.numpy as jnp
from jax import lax
from jax.experimental import pallas as pl
from jax.experimental.pallas import tpu as pltpu
from jax.sharding import PartitionSpec as P

ITERS = 2
NORM_EPS = 1e-05
VEC_EPS = 1e-06

YS, ZS, CS = 4, 8, 2
HALF = ZS // 2
TILE = 512
MESH = pl.DeviceIdType.MESH
F32 = jnp.float32
BF16 = jnp.bfloat16
VMEM_BYTES = 56 * 1024 * 1024
Y_CHUNKS = 2
ROWS_A = 64


def dot(left, right):
    return jnp.dot(left, right, preferred_element_type=F32)


def dot_t(left, right):
    return lax.dot_general(left, right, (((1,), (1,)), ((), ())), preferred_element_type=F32)


def over_tokens(left, right):
    return lax.dot_general(left, right, (((0,), (0,)), ((), ())), preferred_element_type=F32)


def two_parts(wide):
    high = wide.astype(BF16)
    return high, (wide - high.astype(F32)).astype(BF16)


class Refs:
    def __init__(self, names, refs):
        self.__dict__.update(zip(names, refs, strict=True))


class Place:
    def __init__(self, layers):
        self.layers = layers
        self.sec, rep = lax.axis_index("section"), lax.axis_index("replica")
        self.core = lax.rem(rep, CS)
        self.zed = lax.rem(rep // CS, ZS)
        self.why = rep // (CS * ZS)
        self.inner, self.outer = ZS * CS, layers * YS
        self.here, self.there = self.zed * CS + self.core, self.sec * YS + self.why
        self.sibling = self.device(self.sec, self.why, self.zed, 1 - self.core)

    def device(self, sec, why, zed, core):
        return (sec, (why * ZS + zed) * CS + core)

    def y_at(self, step):
        return lax.rem(self.why + step + YS, YS)

    def z_at(self, step):
        return lax.rem(self.zed + step + ZS, ZS)

    def x(self, step):
        return self.device(lax.rem(self.sec + step, self.layers), self.why, self.zed, self.core)

    def y(self, step):
        return self.device(self.sec, self.y_at(step), self.zed, self.core)

    def z(self, step):
        return self.device(self.sec, self.why, self.z_at(step), self.core)

    def near(self, step):
        return (self.sec, self.why * self.inner + lax.rem(self.here + step, self.inner))

    def far(self, step):
        other = lax.rem(self.there + step, self.outer)
        return (other // YS, lax.rem(other, YS) * self.inner + self.here)

    def slot(self, layer):
        return lax.rem(layer - self.sec + self.layers, self.layers)


def greet(partners):
    barrier = pltpu.get_barrier_semaphore()
    for partner in partners:
        pl.semaphore_signal(barrier, inc=1, device_id=partner, device_id_type=MESH)
    pl.semaphore_wait(barrier, len(partners))


def remote(src, dst, send_sem, recv_sem, partner):
    return pltpu.make_async_remote_copy(
        src_ref=src,
        dst_ref=dst,
        send_sem=send_sem,
        recv_sem=recv_sem,
        device_id=partner,
        device_id_type=MESH,
    )


def exchange(sends, count, partner, source, landing, send, recv):
    copies = []
    for step in range(1, count):
        copy = remote(source(step), landing(step), send.at[step - 1], recv.at[step - 1], partner(step))
        copy.start()
        copies.append(copy)
    sends += copies
    return copies


def arrived(ref, send, recv, at, partner):
    remote(ref, ref, send.at[at], recv.at[at], partner).wait_recv()


def drain(sends):
    for copy in sends:
        copy.wait_send()
    sends.clear()


def merged(*threads):
    threads = list(threads)
    while threads:
        for thread in list(threads):
            try:
                next(thread)
            except StopIteration:
                threads.remove(thread)
                continue
            yield


def finish(thread):
    for _ in thread:
        pass


GATHER_KINDS = 12


def gather_sems(blocks):
    first = blocks // 2
    dma = pltpu.SemaphoreType.DMA
    ring, hand = (ZS - 1, first), (ZS, first)
    return [dma((YS - 1,)), dma((YS - 1,)), dma(ring), dma(ring), dma(hand), dma(hand),
            dma((ZS - 1,)), dma((ZS - 1,)), dma((YS,)), dma((YS,)), dma((YS,)), dma((YS,))]


def ring_steps():
    return [(step, way) for step in range(1, HALF + 1) for way in (1, -1) if way > 0 or step < HALF]


def gather_first(out, blocks, at, sems, sends):
    ysend, yrecv, zsend, zrecv, csend, crecv = sems
    mine = out.at[pl.ds(blocks[0], len(blocks)), at.why, at.zed, at.core]
    exchange(sends, YS, at.y, lambda step: mine, lambda step: mine, ysend, yrecv)

    def bundle(chunk, z, core):
        return out.at[blocks[chunk], :, z, core]

    steps = ring_steps()

    def index(step, way):
        return steps.index((step, way))

    def hand_index(step, way):
        return 0 if step == 0 else index(step, way) + 1

    def send(step, way, chunk):
        view = bundle(chunk, at.z_at(-way * (step - 1)), at.core)
        copy = remote(view, view, zsend.at[index(step, way), chunk], zrecv.at[index(step, way), chunk],
                      at.z(way))
        copy.start()
        sends.append(copy)

    def hand_on(step, way, chunk):
        view = bundle(chunk, at.z_at(-way * step), at.core)
        copy = remote(view, view, csend.at[hand_index(step, way), chunk],
                      crecv.at[hand_index(step, way), chunk], at.sibling)
        copy.start()
        sends.append(copy)

    yield
    for step in range(1, YS):
        block = out.at[pl.ds(blocks[0], len(blocks)), at.y_at(-step), at.zed, at.core]
        arrived(block, ysend, yrecv, step - 1, at.sibling)
    for chunk in range(len(blocks)):
        send(1, 1, chunk)
        send(1, -1, chunk)
    for chunk in range(len(blocks)):
        hand_on(0, 1, chunk)
    for step in range(1, HALF + 1):
        for chunk in range(len(blocks)):
            yield
            for way in (1, -1):
                if (step, way) not in steps:
                    continue
                view = bundle(chunk, at.z_at(-way * step), at.core)
                remote(view, view, zsend.at[index(step, way), chunk], zrecv.at[index(step, way), chunk],
                       at.sibling).wait_recv()
                if (step + 1, way) in steps:
                    send(step + 1, way, chunk)
                hand_on(step, way, chunk)
    for step, way in [(0, 1)] + steps:
        yield
        for chunk in range(len(blocks)):
            view = bundle(chunk, at.z_at(-way * step), 1 - at.core)
            remote(view, view, csend.at[hand_index(step, way), chunk],
                   crecv.at[hand_index(step, way), chunk], at.sibling).wait_recv()


def gather_second(out, blocks, at, sems, sends, pauses):
    zsend, zrecv, ysend, yrecv, csend, crecv = sems
    span = pl.ds(blocks[0], len(blocks))

    def view(z):
        return out.at[span, at.why, z, at.core]

    def bundle(step, core, part=None):
        zeds = pl.ds(0, ZS) if part is None else pl.ds(part * HALF, HALF)
        return out.at[span, at.y_at(step), zeds, core]

    def along(ref, idx, way):
        copy = remote(ref, ref, ysend.at[idx], yrecv.at[idx], at.y(way))
        copy.start()
        sends.append(copy)

    def hand_on(step, idx):
        ref = bundle(step, at.core)
        copy = remote(ref, ref, csend.at[idx], crecv.at[idx], at.sibling)
        copy.start()
        sends.append(copy)

    exchange(sends, ZS, at.z, lambda step: view(at.zed), lambda step: view(at.zed), zsend, zrecv)
    for _ in range(pauses[0]):
        yield
    for step in range(1, ZS):
        arrived(view(at.z_at(-step)), zsend, zrecv, step - 1, at.sibling)
    along(bundle(0, at.core), 0, 1)
    along(bundle(0, at.core), 1, -1)
    hand_on(0, 0)
    for _ in range(pauses[1]):
        yield
    arrived(bundle(-1, at.core), ysend, yrecv, 0, at.sibling)
    along(bundle(-1, at.core, 0), 2, 1)
    arrived(bundle(1, at.core), ysend, yrecv, 1, at.sibling)
    along(bundle(1, at.core, 1), 3, -1)
    hand_on(-1, 1)
    hand_on(1, 2)
    for _ in range(pauses[2]):
        yield
    arrived(bundle(2, at.core, 0), ysend, yrecv, 2, at.sibling)
    arrived(bundle(2, at.core, 1), ysend, yrecv, 3, at.sibling)
    hand_on(2, 3)
    for idx, step in enumerate((0, -1, 1, 2)):
        yield
        arrived(bundle(step, 1 - at.core), csend, crecv, idx, at.sibling)


def gather(out, start, count, at, sems, sends):
    half = count // 2
    first = list(range(start, start + half))
    second = list(range(start + half, start + count))
    chunks = len(first)
    pauses = (chunks + 1, 2 * chunks, chunks + 1)
    return merged(gather_second(out, second, at, sems[6:], sends, pauses),
                  gather_first(out, first, at, sems[:6], sends))


def row_block(ref, block, idx):
    per = TILE // (CS * 64)
    wide = ref[block, idx // (ZS // per), pl.ds((idx % (ZS // per)) * per, per)]
    return wide.reshape(TILE, 128)


def tiles(full_d, body, between=None, parts=1):
    def step(idx, carry):
        body(idx, pl.ds(pl.multiple_of(idx * TILE, TILE), TILE))
        return carry
    count = full_d // TILE // parts
    for part in range(parts):
        lax.fori_loop(part * count, (part + 1) * count, step, 0)
        if between is not None:
            between()


def every_up(ref, at, idx):
    return jnp.concatenate(
        [row_block(ref.weights, 2 * at.slot(layer) + 1, idx) for layer in range(at.layers)], axis=1)


def lane_sums(wide):
    return sum(wide[:, start:start + 128] for start in range(0, TILE, 128))


def primal(ref, at, full_d, between):
    layers, sec = at.layers, at.sec
    tokens = ref.rows.shape[0]
    acc, along = ref.acc, ref.along
    along[0] = jnp.zeros((tokens, 128), F32)

    def rows_of(layer, cols):
        return ref.rows[:, cols] if layer == 0 else ref.every_row[layer - 1, :, cols]

    def square(idx, cols):
        wide = ref.rows[:, cols].astype(F32)
        along[0] += lane_sums(wide * wide)
    tiles(full_d, square, between)
    for layer in range(layers):
        down, up = 2 * at.slot(layer), 2 * at.slot(layer) + 1
        mean = jnp.sum(along[0], axis=-1, keepdims=True) * (1.0 / full_d)
        inv = lax.rsqrt(mean + NORM_EPS)
        acc[0] = jnp.zeros((tokens, 128), F32)

        def project(idx, cols):
            gain = ref.gains[at.slot(layer), :, cols]
            piece = (rows_of(layer, cols).astype(F32) * inv * gain).astype(BF16)

            @pl.when(sec == layer)
            def _():
                ref.normed[:, cols] = piece
            acc[0] += dot(piece, row_block(ref.weights, down, idx))
        tiles(full_d, project, between, 2)
        pre = acc[0]
        sig = jax.nn.sigmoid(pre)
        act = (pre * sig).astype(BF16)
        ref.hidden[:, layer * 128:(layer + 1) * 128] = act

        @pl.when(sec == layer)
        def _():
            ref.own_hidden[...] = act
        ref.pre_act[layer] = pre
        ref.slope[layer] = sig + pre * sig * (1.0 - sig)
        ref.inv_rms[layer] = jnp.broadcast_to(inv, (tokens, 128))
        along[0] = jnp.zeros((tokens, 128), F32)
        if layer + 1 < layers:
            def forward(idx, cols):
                wide = rows_of(layer, cols).astype(F32)
                wide = wide + dot_t(act, row_block(ref.weights, up, idx))
                rounded = wide.astype(BF16)
                ref.every_row[layer, :, cols] = rounded
                again = rounded.astype(F32)
                along[0] += lane_sums(again * again)
            tiles(full_d, forward, between, 2)
    ref.gram[...] = over_tokens(ref.hidden[...], ref.own_hidden[...])
    between()


def weight_products(ref, at, full_d, between):
    layers, sec = at.layers, at.sec
    part = ref.rows.shape[0] // layers
    mine = pl.ds(pl.multiple_of(sec * part, part), part)
    ref.uu[...] = jnp.zeros_like(ref.uu)
    ref.ud[...] = jnp.zeros_like(ref.ud)
    ref.row_up[...] = jnp.zeros_like(ref.row_up)

    def grams(idx, cols):
        every = every_up(ref, at, idx)
        turned = every.T
        ref.uu[...] += dot(turned, every)
        pair_at = 0
        for layer in range(1, layers):
            width = layer * 128
            gain = ref.gains[at.slot(layer), :, cols]
            high, low = two_parts(turned[:width].astype(F32) * gain)
            down = row_block(ref.weights, 2 * at.slot(layer), idx)
            pair = dot(high, down) + dot(low, down)
            block = dot(ref.every_row[layer - 1, mine, cols], every[:, :width])
            for k in range(layer):
                ref.ud[pair_at] += pair[k * 128:(k + 1) * 128]
                ref.row_up[pair_at] += block[:, k * 128:(k + 1) * 128]
                pair_at += 1
    tiles(full_d, grams, between, 4)
    ref.uu_high[...], ref.uu_low[...] = two_parts(ref.uu[...])
    ref.ud_high[...], ref.ud_low[...] = two_parts(ref.ud[...])


def recurrence(tan_base, back_base, pre_act, slope, inv_rms, row_up, up_up, up_down, full_d):
    layers = len(tan_base)
    tan_act = []
    for layer in range(layers):
        tan_pre = tan_base[layer]
        if layer > 0:
            moved = sum(dot(tan_act[k], up_down[k][layer][0]) + dot(tan_act[k], up_down[k][layer][1])
                        for k in range(layer))
            along = sum(jnp.sum(tan_act[k].astype(F32) * row_up[layer][k], axis=-1, keepdims=True)
                        for k in range(layer))
            inv = inv_rms[layer]
            tan_pre = tan_pre + inv * moved - (inv * inv * (1.0 / full_d)) * along * pre_act[layer]
        tan_act.append((tan_pre * slope[layer]).astype(BF16))
    every = jnp.concatenate(tan_act, axis=1)
    back_all = dot(every, up_up[0]) + dot(every, up_up[1])
    back_pre, moved_back, pull = {}, {}, {}
    for layer in reversed(range(layers)):
        back_act = back_base[layer] + back_all[:, layer * 128:(layer + 1) * 128]
        for k in range(layer + 1, layers):
            back_act = back_act + dot_t(moved_back[k], up_down[layer][k][0])
            back_act = back_act + dot_t(moved_back[k], up_down[layer][k][1])
            back_act = back_act - pull[k] * row_up[k][layer]
        piece = (back_act * slope[layer]).astype(BF16)
        wide = piece.astype(F32)
        inv = inv_rms[layer]
        back_pre[layer] = piece
        moved_back[layer] = (wide * inv).astype(BF16)
        pull[layer] = inv * inv * (1.0 / full_d) * jnp.sum(wide * pre_act[layer], axis=-1, keepdims=True)
    return tan_act + [back_pre[layer] for layer in range(layers)]


def token_terms(ref, at, full_d):
    layers, sec = at.layers, at.sec
    acc, along = ref.acc, ref.along
    acc[...] = jnp.zeros_like(acc)
    ref.acc_up[...] = jnp.zeros_like(ref.acc_up)
    along[...] = jnp.zeros_like(along)
    own_hidden = ref.own_hidden[...]
    part = own_hidden.shape[0] // layers

    def body(idx, cols):
        acc[0] += dot(ref.normed[:, cols], row_block(ref.vector, 0, idx))
        spread = dot_t(own_hidden, row_block(ref.vector, 1, idx))
        rounded = spread.astype(BF16)
        ref.acc_up[...] += dot(rounded, every_up(ref, at, idx))
        for layer in range(1, layers):
            scaled = (spread * ref.gains[at.slot(layer), :, cols]).astype(BF16)
            acc[layer] += dot(scaled, row_block(ref.weights, 2 * at.slot(layer), idx))
            along[layer] += lane_sums(ref.every_row[layer - 1, :, cols].astype(F32) * spread)
    tiles(full_d, body)
    base = acc[0]

    def put(block, value):
        value = value.astype(BF16)
        for quarter in range(layers):
            ref.pay[quarter, :, block * 128:(block + 1) * 128] = value[quarter * part:(quarter + 1) * part]
    for layer in range(layers):
        own = jnp.where(sec == layer, base, 0.0)
        if layer > 0:
            inv = ref.inv_rms[layer]
            reach = jnp.sum(along[layer], axis=-1, keepdims=True)
            later = inv * acc[layer] - (inv * inv * (1.0 / full_d)) * reach * ref.pre_act[layer]
            own = own + jnp.where(sec < layer, later, 0.0)
        put(layer, own)
        put(layers + layer, ref.acc_up[:, layer * 128:(layer + 1) * 128])


def gradient_terms(ref, at, full_d):
    layers, sec = at.layers, at.sec
    res = ref.result
    part = res.shape[1]
    tokens = part * layers

    def column(block):
        return jnp.concatenate([res[q, :, block * 128:(block + 1) * 128] for q in range(layers)], axis=0)
    back = [column(layers + layer) for layer in range(layers)]
    pulls, moved = [], []
    for layer in range(layers):
        inv = ref.inv_rms[layer]
        wide = back[layer].astype(F32)
        pull = inv * inv * (1.0 / full_d) * jnp.sum(wide * ref.pre_act[layer], axis=-1, keepdims=True)
        pulls.append(jnp.where(sec < layer, pull, 0.0))
        moved.append(jnp.where(sec < layer, wide * inv, 0.0).astype(BF16))
    acts = []
    later = jnp.zeros((tokens, 128), F32)
    for layer in reversed(range(layers)):
        old = ref.hidden[:, layer * 128:(layer + 1) * 128].astype(F32)
        acts.insert(0, (column(layer).astype(F32) - later * old).astype(BF16))
        later = later + pulls[layer]
    total = later[:, :1]
    act_cat = jnp.concatenate(acts, axis=1)
    own_back = back[0]
    for layer in range(1, layers):
        own_back = jnp.where(sec == layer, back[layer], own_back)
    own_hidden = ref.own_hidden[...]
    per = TILE // (CS * 64)

    def body(idx, cols):
        cot = dot_t(act_cat, every_up(ref, at, idx)) - total * ref.rows[:, cols].astype(F32)
        for layer in range(1, layers):
            cot = cot + (dot_t(moved[layer], row_block(ref.weights, 2 * at.slot(layer), idx))
                         * ref.gains[at.slot(layer), :, cols])
        where = (idx // (ZS // per), pl.ds((idx % (ZS // per)) * per, per))
        up = over_tokens(cot.astype(BF16), own_hidden).reshape(per, CS, 64, 128)
        down = over_tokens(ref.normed[:, cols], own_back).reshape(per, CS, 64, 128)
        ref.part[where] = jnp.concatenate([down, up], axis=2)
        swap_copy(ref, at, idx).start()
    tiles(full_d, body)


def swap_copy(ref, at, idx):
    per = TILE // (CS * 64)
    where = (idx // (ZS // per), pl.ds((idx % (ZS // per)) * per, per))
    return remote(ref.part.at[where + (1 - at.core,)], ref.swap.at[where], ref.swap_send.at[idx],
                  ref.swap_recv.at[idx], at.sibling)


def scatter_first(ref, at, sends, done):
    left_in, right_in, y_in = ref.left_in, ref.right_in, ref.y_a
    size = YS // Y_CHUNKS

    def chunk_of(chunk):
        return pl.ds(chunk * size, size)

    def chip_sum(z, chunk):
        span = chunk_of(chunk)
        return ref.swap[span, z, :ROWS_A] + ref.part[span, z, at.core, :ROWS_A]

    def left(step, chunk):
        z = at.z_at(step - HALF - 1)
        return remote(ref.out_a.at[chunk_of(chunk), z], left_in.at[step - 1, chunk_of(chunk)],
                      ref.ls.at[step - 1, chunk], ref.lr.at[step - 1, chunk], at.z(-1))

    def right(step, chunk):
        z = at.z_at(HALF - step)
        return remote(ref.out_a.at[chunk_of(chunk), z], right_in.at[step - 1, chunk_of(chunk)],
                      ref.rs.at[step - 1, chunk], ref.rr.at[step - 1, chunk], at.z(1))

    def go(copy):
        copy.start()
        sends.append(copy)

    for step in range(1, HALF + 1):
        for chunk in range(Y_CHUNKS):
            if step > 1:
                yield
            span = chunk_of(chunk)
            z = at.z_at(step - HALF - 1)
            value = chip_sum(z, chunk)
            if step > 1:
                left(step - 1, chunk).wait_recv()
                value = value + left_in[step - 2, span]
            ref.out_a[span, z] = value
            go(left(step, chunk))
            if step < HALF:
                z = at.z_at(HALF - step)
                value = chip_sum(z, chunk)
                if step > 1:
                    right(step - 1, chunk).wait_recv()
                    value = value + right_in[step - 2, span]
                ref.out_a[span, z] = value
                go(right(step, chunk))
    yield
    for chunk in range(Y_CHUNKS):
        span = chunk_of(chunk)
        value = chip_sum(at.zed, chunk)
        right(HALF - 1, chunk).wait_recv()
        value = value + right_in[HALF - 2, span]
        left(HALF, chunk).wait_recv()
        ref.out_a[span, at.zed] = value + left_in[HALF - 1, span]

    copies = exchange(sends, YS, at.y, lambda step: ref.out_a.at[at.y_at(step), at.zed],
                      lambda step: y_in.at[step - 1], ref.yas, ref.yar)
    yield
    value = ref.out_a[at.why, at.zed]
    for step, copy in enumerate(copies):
        copy.wait_recv()
        value = value + y_in[step]
    done.append(value)


def scatter_second(ref, at, sends, done):
    halves = (pl.ds(0, HALF), pl.ds(HALF, HALF))
    out = ref.out_b

    def chip_sum(step, half):
        y = at.y_at(step)
        return ref.swap[y, halves[half], ROWS_A:] + ref.part[y, halves[half], at.core, ROWS_A:]

    def go(src, dst, idx, way):
        copy = remote(src, dst, ref.ybs.at[idx], ref.ybr.at[idx], at.y(way))
        copy.start()
        sends.append(copy)

    def took(dst, idx):
        arrived(dst, ref.ybs, ref.ybr, idx, at.sibling)

    def view(step, half):
        return out.at[at.y_at(step), halves[half]]

    out[at.y_at(2), halves[0]] = chip_sum(2, 0)
    go(view(2, 0), ref.chain.at[0], 0, 1)
    out[at.y_at(2), halves[1]] = chip_sum(2, 1)
    go(view(2, 1), ref.chain.at[1], 1, -1)
    out[at.y_at(1), halves[1]] = chip_sum(1, 1)
    go(view(1, 1), ref.from_low.at[halves[1]], 2, 1)
    out[at.y_at(-1), halves[0]] = chip_sum(-1, 0)
    go(view(-1, 0), ref.from_high.at[halves[0]], 3, -1)
    yield
    yield
    took(ref.chain.at[0], 0)
    out[at.y_at(1), halves[0]] = chip_sum(1, 0) + ref.chain[0]
    go(view(1, 0), ref.from_low.at[halves[0]], 4, 1)
    took(ref.chain.at[1], 1)
    out[at.y_at(-1), halves[1]] = chip_sum(-1, 1) + ref.chain[1]
    go(view(-1, 1), ref.from_high.at[halves[1]], 5, -1)
    yield
    yield
    yield
    took(ref.from_low.at[halves[1]], 2)
    took(ref.from_high.at[halves[0]], 3)
    took(ref.from_low.at[halves[0]], 4)
    took(ref.from_high.at[halves[1]], 5)
    for half in range(2):
        out[at.why, halves[half]] = (
            chip_sum(0, half) + ref.from_low[halves[half]] + ref.from_high[halves[half]])
    copies = exchange(sends, ZS, at.z, lambda step: out.at[at.why, at.z_at(step)],
                      lambda step: ref.z_b.at[step - 1], ref.zbs, ref.zbr)
    yield
    yield
    yield
    value = out[at.why, at.zed]
    for step, copy in enumerate(copies):
        copy.wait_recv()
        value = value + ref.z_b[step]
    done.append(value)


def scatter_sum(ref, at, full_d, sends):
    for idx in range(full_d // TILE):
        copy = swap_copy(ref, at, idx)
        copy.wait_recv()
        sends.append(copy)
    done_a, done_b = [], []
    finish(merged(scatter_second(ref, at, sends, done_b), scatter_first(ref, at, sends, done_a)))
    both = jnp.concatenate([done_a[0], done_b[0]], axis=0)
    return both[:64], both[64:]


def gram_steps(ref, at, sends):
    gram, whole = ref.gram, ref.hidden_gram
    piece = gram.shape[0] // at.inner
    small = piece // YS

    def rows(index, size):
        return pl.ds(pl.multiple_of(index * size, size), size)

    copies = exchange(sends, at.inner, at.near,
                      lambda step: gram.at[rows(lax.rem(at.here + step, at.inner), piece)],
                      lambda step: ref.gram_in.at[step - 1], ref.g1s, ref.g1r)
    yield
    value = gram[rows(at.here, piece), :]
    for step, copy in enumerate(copies):
        copy.wait_recv()
        value = value + ref.gram_in[step]
    ref.gram_sum[...] = value
    copies = exchange(sends, YS, at.y, lambda step: ref.gram_sum.at[rows(at.y_at(step), small)],
                      lambda step: ref.gram_in2.at[step - 1], ref.g2s, ref.g2r)
    yield
    own = rows(at.why, small)
    value = ref.gram_sum[own, :]
    for step, copy in enumerate(copies):
        copy.wait_recv()
        value = value + ref.gram_in2[step]
    ref.gram_out[own, :] = value
    exchange(sends, YS, at.y, lambda step: ref.gram_out.at[own], lambda step: ref.gram_out.at[own],
             ref.g3s, ref.g3r)
    yield
    for step in range(1, YS):
        arrived(ref.gram_out.at[rows(at.y_at(-step), small)], ref.g3s, ref.g3r, step - 1, at.sibling)
    mine = rows(at.here, piece)
    whole[mine, :] = ref.gram_out[...]
    exchange(sends, at.inner, at.near, lambda step: ref.gram_out, lambda step: whole.at[mine],
             ref.g4s, ref.g4r)
    yield
    for step in range(1, at.inner):
        source = rows(lax.rem(at.here + at.inner - step, at.inner), piece)
        arrived(whole.at[source], ref.g4s, ref.g4r, step - 1, at.sibling)


def sum_all(ref, at, line, sends):
    vec, near, far, half_sum = ref.vec, ref.near, ref.far, ref.half_sum
    vec[...] = jnp.broadcast_to(line, vec.shape)
    exchange(sends, at.inner, at.near, lambda step: vec, lambda step: near.at[at.here], ref.ns, ref.nr)
    near[at.here] = vec[...]
    for step in range(1, at.inner):
        slot = near.at[lax.rem(at.here + at.inner - step, at.inner)]
        arrived(slot, ref.ns, ref.nr, step - 1, at.sibling)
    half_sum[...] = jnp.sum(near[...], axis=0)
    exchange(sends, at.outer, at.far, lambda step: half_sum, lambda step: far.at[at.there], ref.fs, ref.fr)
    far[at.there] = half_sum[...]
    for step in range(1, at.outer):
        slot = far.at[lax.rem(at.there + at.outer - step, at.outer)]
        arrived(slot, ref.fs, ref.fr, step - 1, at.sibling)
    return jnp.sum(far[...], axis=0)[:1]


def put_vector(ref, at, down_rows, up_rows, full_d, rank, sends):
    ref.shard[0] = (down_rows * (full_d ** -0.5)).astype(BF16)
    ref.shard[1] = (up_rows * (rank ** -0.5)).astype(BF16)
    ref.vector[:, at.why, at.zed, at.core] = ref.shard[...]
    ref.ups[0] = ref.shard[1]
    exchange(sends, at.layers, at.x, lambda step: ref.shard.at[1],
             lambda step: ref.ups.at[at.layers - step], ref.x3s, ref.x3r)


def ups_arrived(ref, at):
    for step in range(1, at.layers):
        arrived(ref.ups.at[at.layers - step], ref.x3s, ref.x3r, step - 1, at.sibling)


def curvature(ref, at, full_d, sends, between):
    layers, sec = at.layers, at.sec
    token_terms(ref, at, full_d)
    pay = ref.pay
    copies = exchange(sends, layers, at.x, lambda step: pay.at[lax.rem(sec + step, layers)],
                      lambda step: ref.pay_in.at[step - 1], ref.x1s, ref.x1r)
    total = pay[sec].astype(F32)
    for step, copy in enumerate(copies):
        copy.wait_recv()
        total = total + ref.pay_in[step].astype(F32)
    between()
    row_up = {}
    up_down = {k: {} for k in range(layers)}
    idx = 0
    for layer in range(layers):
        for k in range(layer):
            row_up.setdefault(layer, {})[k] = ref.row_up[idx]
            up_down[k][layer] = (ref.ud_high[idx], ref.ud_low[idx])
            idx += 1
    part = pay.shape[1]
    mine = pl.ds(pl.multiple_of(sec * part, part), part)
    pieces = recurrence(
        [total[:, start * 128:(start + 1) * 128] for start in range(layers)],
        [total[:, start * 128:(start + 1) * 128] for start in range(layers, 2 * layers)],
        [ref.pre_act[layer, mine, :] for layer in range(layers)],
        [ref.slope[layer, mine, :] for layer in range(layers)],
        [ref.inv_rms[layer, mine, :] for layer in range(layers)],
        row_up, (ref.uu_high[...], ref.uu_low[...]), up_down, full_d)
    result = ref.result
    result[sec] = jnp.concatenate(pieces, axis=1)
    own = result.at[sec]
    exchange(sends, layers, at.x, lambda step: own, lambda step: own, ref.x2s, ref.x2r)
    between()
    for step in range(1, layers):
        arrived(result.at[lax.rem(sec + layers - step, layers)], ref.x2s, ref.x2r, step - 1, at.sibling)
    between()
    gradient_terms(ref, at, full_d)
    return scatter_sum(ref, at, full_d, sends)


def main_kernel(cfg, names, *refs):
    layers, tokens_all, base_count = cfg
    ref = Refs(names, refs)
    at = Place(layers)
    full_d, rank = ref.rows.shape[1], ref.down.shape[-1]
    sends = []
    lane = lax.broadcasted_iota(jnp.int32, (1, 128), 1)
    copies = [pltpu.make_async_copy(ref.down, ref.weights.at[0], ref.local.at[0]),
              pltpu.make_async_copy(ref.up, ref.weights.at[1], ref.local.at[1])]
    for copy in copies:
        copy.start()
    ref.gains[0] = ref.gain[...]
    greet([at.near(step) for step in range(1, at.inner)] + [at.far(step) for step in range(1, at.outer)])

    for block, source in enumerate((ref.down, ref.up)):
        row = source.at[at.why, at.zed, at.core]
        exchange(sends, layers, at.x, lambda step: row,
                 lambda step: ref.weights.at[2 * (layers - step) + block, at.why, at.zed, at.core],
                 ref.xws.at[block], ref.xwr.at[block])
    exchange(sends, layers, at.x, lambda step: ref.gain, lambda step: ref.gains.at[layers - step],
             ref.xgs, ref.xgr)
    put_vector(ref, at, ref.basis[base_count - 1, 0], ref.basis[base_count - 1, 1], full_d, rank, sends)
    for step in range(1, layers):
        for block in range(2):
            arrived(ref.weights.at[2 * (layers - step) + block, at.why, at.zed, at.core],
                    ref.xws.at[block], ref.xwr.at[block], step - 1, at.sibling)
    sems = [ref.__dict__[key] for key in range(2 * GATHER_KINDS)]
    finish(gather(ref.weights, 2, 2 * layers - 2, at, sems[:GATHER_KINDS], sends))
    for step in range(1, layers):
        arrived(ref.gains.at[layers - step], ref.xgs, ref.xgr, step - 1, at.sibling)
    for copy in copies:
        copy.wait()
    moving = gather(ref.vector, 0, 2, at, sems[GATHER_KINDS:], sends)

    calls = []

    def move():
        calls.append(None)
        if len(calls) % 2 == 0:
            next(moving, None)
    next(moving, None)
    next(moving, None)
    primal(ref, at, full_d, move)
    weight_products(ref, at, full_d, move)
    finish(moving)
    ups_arrived(ref, at)
    drain(sends)

    norm = 1.0 / tokens_all
    scales = (full_d ** -0.5, rank ** -0.5)
    held = [(ref.basis[k, 0], ref.basis[k, 1]) for k in range(base_count)]
    gram_slots = {}

    def gram_at(k, j):
        return gram_slots[max(k, j), min(k, j)]

    def inner_sum(left, right):
        both = left[0] * right[0] + left[1] * right[1]
        return jnp.sum(jnp.sum(both, axis=0, keepdims=True), axis=1, keepdims=True)

    for it in range(ITERS):
        count = base_count + it
        summing = gram_steps(ref, at, sends) if it == 0 else iter(())
        next(summing, None)
        sum_a, sum_b = curvature(ref, at, full_d, sends, lambda: next(summing, None))
        finish(summing)
        for layer in range(layers):
            wide = ref.hidden_gram[layer * rank:(layer + 1) * rank, :]
            high = wide.astype(BF16)
            rest = wide - high.astype(F32)
            middle, low = two_parts(rest)
            ups = ref.ups[at.slot(layer)]
            sum_b = sum_b + dot(ups, high) + dot(ups, middle) + dot(ups, low)
        image = [sum_a * (scales[0] * norm), sum_b * (scales[1] * norm)]

        pairs = [(k, j) for k in range(count) for j in range(k + 1) if (k, j) not in gram_slots]
        values = [inner_sum(item, image) for item in held] + [inner_sum(image, image)]
        values += [inner_sum(held[k], held[j]) for k, j in pairs]
        line = jnp.zeros((1, 128), F32)
        for place, value in enumerate(values):
            line = jnp.where(lane == place, value, line)
        line = sum_all(ref, at, line, sends) * (1.0 / (layers * 2 * full_d * rank))
        totals = [jnp.sum(jnp.where(lane == place, line, 0.0), axis=1, keepdims=True)
                  for place in range(len(values))]
        first_coef, image_square = totals[:count], totals[count]
        gram_slots.update(zip(pairs, totals[count + 1:]))
        coef, length_square = [], image_square
        for k in range(count):
            again = sum(gram_at(k, j) * first_coef[j] for j in range(count))
            coef.append(first_coef[k] + (first_coef[k] - again))
        for k in range(count):
            mixed = sum(gram_at(k, j) * coef[j] for j in range(count))
            length_square = length_square + coef[k] * (mixed - 2.0 * first_coef[k])
        length = jnp.sqrt(jnp.maximum(length_square, 0.0) + VEC_EPS)
        fresh = []
        for block in range(2):
            clean = image[block]
            for k in range(count):
                clean = clean - coef[k] * held[k][block]
            fresh.append(clean / length)
            ref.fresh[it, block] = fresh[block]
        line = jnp.zeros((1, 128), F32)
        for k in range(count):
            line = jnp.where(lane == k, coef[k], line)
        line = jnp.where(lane == base_count + ITERS, length, line)
        ref.hess[it:it + 1, :] = line[:, :base_count + ITERS + 1]
        drain(sends)
        if it + 1 < ITERS:
            held.append((ref.fresh[it, 0], ref.fresh[it, 1]))
            put_vector(ref, at, fresh[0], fresh[1], full_d, rank, sends)
            finish(gather(ref.vector, 0, 2, at, sems[GATHER_KINDS:], sends))
            ups_arrived(ref, at)
            drain(sends)


def per_device(hidden_in, down_weight, up_weight, norm_gain, krylov_basis):
    layers = lax.axis_size("section")
    micro, tok, full_d = hidden_in.shape
    rank = down_weight.shape[2]
    tokens = micro * tok
    part = tokens // layers
    basis = krylov_basis[:, 0]
    base_count, _, rows, _ = basis.shape
    split = (YS, ZS, CS, rows, rank)
    vmem = pl.BlockSpec(memory_space=pltpu.VMEM)
    hbm = pl.BlockSpec(memory_space=pl.ANY)
    dma = pltpu.SemaphoreType.DMA
    inner, outer = ZS * CS, layers * YS
    pairs = layers * (layers - 1) // 2
    wide = layers * rank
    piece = wide // inner
    rows_b = 2 * rows - ROWS_A

    inputs = dict(
        rows=hidden_in.reshape(tokens, full_d),
        down=down_weight[0].reshape(split),
        up=up_weight[0].reshape(split),
        gain=norm_gain,
        basis=basis,
    )
    outputs = dict(
        fresh=jax.ShapeDtypeStruct((ITERS, 2, rows, rank), F32),
        hess=jax.ShapeDtypeStruct((ITERS, base_count + ITERS + 1), F32),
    )
    scratch = dict(
        weights=pltpu.VMEM((2 * layers,) + split, BF16),
        vector=pltpu.VMEM((2,) + split, BF16),
        gains=pltpu.VMEM((layers, 1, full_d), F32),
        ups=pltpu.VMEM((layers, rows, rank), BF16),
        shard=pltpu.VMEM((2, rows, rank), BF16),
        every_row=pltpu.VMEM((layers - 1, tokens, full_d), BF16),
        normed=pltpu.VMEM((tokens, full_d), BF16),
        hidden=pltpu.VMEM((tokens, wide), BF16),
        own_hidden=pltpu.VMEM((tokens, rank), BF16),
        pre_act=pltpu.VMEM((layers, tokens, rank), F32),
        slope=pltpu.VMEM((layers, tokens, rank), F32),
        inv_rms=pltpu.VMEM((layers, tokens, 128), F32),
        row_up=pltpu.VMEM((pairs, part, rank), F32),
        uu=pltpu.VMEM((wide, wide), F32),
        ud=pltpu.VMEM((pairs, rank, rank), F32),
        uu_high=pltpu.VMEM((wide, wide), BF16),
        uu_low=pltpu.VMEM((wide, wide), BF16),
        ud_high=pltpu.VMEM((pairs, rank, rank), BF16),
        ud_low=pltpu.VMEM((pairs, rank, rank), BF16),
        gram=pltpu.VMEM((wide, rank), F32),
        hidden_gram=pltpu.VMEM((wide, rank), F32),
        gram_in=pltpu.VMEM((inner - 1, piece, rank), F32),
        gram_sum=pltpu.VMEM((piece, rank), F32),
        gram_in2=pltpu.VMEM((YS - 1, piece // YS, rank), F32),
        gram_out=pltpu.VMEM((piece, rank), F32),
        acc=pltpu.VMEM((layers, tokens, rank), F32),
        acc_up=pltpu.VMEM((tokens, wide), F32),
        along=pltpu.VMEM((layers, tokens, 128), F32),
        pay=pltpu.VMEM((layers, part, 2 * wide), BF16),
        pay_in=pltpu.VMEM((layers - 1, part, 2 * wide), BF16),
        result=pltpu.VMEM((layers, part, 2 * wide), BF16),
        part=pltpu.VMEM((YS, ZS, CS, 2 * rows, rank), F32),
        swap=pltpu.VMEM((YS, ZS, 2 * rows, rank), F32),
        out_a=pltpu.VMEM((YS, ZS, ROWS_A, rank), F32),
        out_b=pltpu.VMEM((YS, ZS, rows_b, rank), F32),
        left_in=pltpu.VMEM((HALF, YS, ROWS_A, rank), F32),
        right_in=pltpu.VMEM((HALF - 1, YS, ROWS_A, rank), F32),
        y_a=pltpu.VMEM((YS - 1, ROWS_A, rank), F32),
        chain=pltpu.VMEM((2, HALF, rows_b, rank), F32),
        from_low=pltpu.VMEM((ZS, rows_b, rank), F32),
        from_high=pltpu.VMEM((ZS, rows_b, rank), F32),
        z_b=pltpu.VMEM((ZS - 1, rows_b, rank), F32),
        vec=pltpu.VMEM((8, 128), F32),
        near=pltpu.VMEM((inner, 8, 128), F32),
        far=pltpu.VMEM((outer, 8, 128), F32),
        half_sum=pltpu.VMEM((8, 128), F32),
        local=dma((2,)),
        xws=dma((2, layers - 1)), xwr=dma((2, layers - 1)),
        xgs=dma((layers - 1,)), xgr=dma((layers - 1,)),
        x1s=dma((layers - 1,)), x1r=dma((layers - 1,)),
        x2s=dma((layers - 1,)), x2r=dma((layers - 1,)),
        x3s=dma((layers - 1,)), x3r=dma((layers - 1,)),
        g1s=dma((inner - 1,)), g1r=dma((inner - 1,)),
        g2s=dma((YS - 1,)), g2r=dma((YS - 1,)),
        g3s=dma((YS - 1,)), g3r=dma((YS - 1,)),
        g4s=dma((inner - 1,)), g4r=dma((inner - 1,)),
        swap_send=dma((full_d // TILE,)), swap_recv=dma((full_d // TILE,)),
        ls=dma((HALF, Y_CHUNKS)), lr=dma((HALF, Y_CHUNKS)),
        rs=dma((HALF - 1, Y_CHUNKS)), rr=dma((HALF - 1, Y_CHUNKS)),
        yas=dma((YS - 1,)), yar=dma((YS - 1,)),
        ybs=dma((6,)), ybr=dma((6,)),
        zbs=dma((ZS - 1,)), zbr=dma((ZS - 1,)),
        ns=dma((inner - 1,)), nr=dma((inner - 1,)),
        fs=dma((outer - 1,)), fr=dma((outer - 1,)),
    )
    scratch.update(enumerate(gather_sems(2 * layers - 2) + gather_sems(2)))
    names = list(inputs) + list(outputs) + list(scratch)
    cfg = (layers, tokens * lax.axis_size("replica"), base_count)
    fresh, hess = pl.pallas_call(
        functools.partial(main_kernel, cfg, names),
        out_shape=tuple(outputs.values()),
        in_specs=[vmem, hbm, hbm, vmem, vmem],
        out_specs=(vmem, vmem),
        scratch_shapes=list(scratch.values()),
        compiler_params=pltpu.CompilerParams(
            collective_id=1, has_side_effects=True, vmem_limit_bytes=VMEM_BYTES),
    )(*inputs.values())
    return fresh[:, None], hess


def solution(mesh):
    return jax.shard_map(
        per_device,
        mesh=mesh,
        in_specs=(
            P(None, "replica", None),
            P("section", None, None),
            P("section", None, None),
            P("section", None),
            P(None, "section", None, "replica", None),
        ),
        out_specs=(P(None, "section", None, "replica", None), P()),
        check_vma=False,
    )
```
